32 devices in a mesh: row: 8 (over z, core), col: 4 (over y, x).
Axes of the slice: x: 2, y: 2, z: 4, core: 2. Of those that a mesh axis runs over, the one named last changes fastest.
Arguments:
- tiles: bfloat16 [8, 4, 16, 512, 512], P('row', 'col'), as said below
- tile_rows: int32 [8, 4, 16], P('row', 'col'), may hold values from 0 to 11, as said below
- tile_cols: int32 [8, 4, 16], P('row', 'col'), may hold values from 0 to 11
- tile_counts: int32 [8, 4], P('row', 'col'), may hold values from 4 to 16, as said below
- sketch: bfloat16 [49152, 256], P(('row', 'col')), as said below
Outputs:
- basis: float32 [49152, 256], P(('row', 'col'))
- factor: float32 [256, 256], replicated
The draws below stay inside these ranges and needn't reach their ends.
Inputs may be any that keep to these rules, and one draw needn't show every extreme that they name: Within one device's slots the pairs (tile_rows, tile_cols) are all different. `tile_counts`: some device uses all 16 slots in every draw. `tiles`: real valued tile entries of order one over the square root of a row's fan-in. `sketch`: real valued entries of order one.
All inputs are finite; a program needn't handle non-finite values.
Results may differ from the reference program's by a relative error of at most 0.0023.
Values may be sent and summed in bfloat16 or wider, within the bound.
No kernel may reach another device: no remote copies, remote signals or barrier semaphores. Data moves between devices by JAX's collectives and lax.ppermute only.
A program may use at most 64 MiB of HBM per device.

```python
import math
import jax
import jax.numpy as jnp
from jax import lax

TILE = 512
K = 256
BR = 12
BC = 12
CAP = 16
ROW_GROUPS = 8
COL_GROUPS = 4
ROWS = 49152
COLS = 24576


def draw_tiles(key, part):
    shape = (ROW_GROUPS, COL_GROUPS, CAP, TILE, TILE)
    noise_key, scale_key = jax.random.split(jax.random.fold_in(key, 11))
    values = jnp.clip(jax.random.normal(noise_key, shape, jnp.float32), -5.0, 5.0)
    row_scale = jnp.exp(jax.random.uniform(scale_key, (ROW_GROUPS, COL_GROUPS, CAP, TILE, 1), jnp.float32, 0.0, math.log(10.0)))
    fan_width = TILE * CAP * COL_GROUPS // BR
    return (values * row_scale / (4.6 * math.sqrt(fan_width))).astype(jnp.bfloat16)


def tile_layout(key):
    device_keys = jax.random.split(jax.random.fold_in(key, 5), ROW_GROUPS * COL_GROUPS)
    orders = jax.vmap(lambda one_key: jax.random.permutation(one_key, BR * BC))(device_keys)[:, :CAP]
    return orders.reshape(ROW_GROUPS, COL_GROUPS, CAP).astype(jnp.int32)


def draw_tile_rows(key, part):
    return tile_layout(key) // BC


def draw_tile_cols(key, part):
    return tile_layout(key) % BC


def draw_tile_counts(key, part):
    count_key, pick_key = jax.random.split(jax.random.fold_in(key, 17))
    counts = jax.random.randint(count_key, (ROW_GROUPS * COL_GROUPS,), max(1, CAP // 4), CAP + 1, jnp.int32)
    chosen = jax.random.randint(pick_key, (), 0, ROW_GROUPS * COL_GROUPS, jnp.int32)
    counts = counts.at[chosen].set(CAP)
    return counts.reshape(ROW_GROUPS, COL_GROUPS)


def draw_sketch(key, part):
    noise_key, scale_key = jax.random.split(jax.random.fold_in(key, 23), 2)
    column_scale = jnp.exp(jax.random.uniform(scale_key, (1, K), jnp.float32, 0.0, math.log(10.0)))
    values = jnp.clip(jax.random.normal(noise_key, (ROWS, K), jnp.float32), -5.0, 5.0)
    return (values * column_scale / 4.6).astype(jnp.bfloat16)


def setup_inputs(seed: int = 0) -> dict:
    seeds = jax.random.split(jax.random.key(seed), 6)
    tiles = draw_tiles(jax.random.fold_in(seeds[5], 71), 0)
    tile_rows = draw_tile_rows(jax.random.fold_in(seeds[5], 71), 0)
    tile_cols = draw_tile_cols(jax.random.fold_in(seeds[5], 71), 0)
    tile_counts = draw_tile_counts(jax.random.fold_in(seeds[5], 71), 0)
    sketch = draw_sketch(jax.random.fold_in(seeds[5], 71), 0)
    return {"tiles": tiles, "tile_rows": tile_rows, "tile_cols": tile_cols, "tile_counts": tile_counts, "sketch": sketch}


def reference(tiles, tile_rows, tile_cols, tile_counts, sketch):
    tile_size = tiles.shape[-1]
    sketch_width = sketch.shape[1]
    slot_count = tiles.shape[2]
    group_cols = tiles.shape[1]
    flat_tiles = tiles.reshape(-1, tile_size, tile_size)
    tile_total = flat_tiles.shape[0]
    rows_flat = tile_rows.reshape(-1).astype(jnp.int32)
    cols_flat = tile_cols.reshape(-1).astype(jnp.int32)
    counts = tile_counts.reshape(-1).astype(jnp.int32)

    def coords(position):
        position = position.astype(jnp.int32)
        device = position // slot_count
        slot_number = position % slot_count
        row_group = device // group_cols
        col_group = device % group_cols
        live_mask = (slot_number < counts[device]).astype(jnp.float32)
        row_start = ((row_group * BR + rows_flat[position]) * tile_size).astype(jnp.int32)
        col_start = ((col_group * BC + cols_flat[position]) * tile_size).astype(jnp.int32)
        matrix = lax.dynamic_index_in_dim(flat_tiles, position, 0, keepdims=False)
        return (matrix, live_mask, row_start, col_start)

    def first_pass(position, running):
        matrix, live_mask, row_start, col_start = coords(position)
        sketch_block = lax.dynamic_slice_in_dim(sketch, row_start, tile_size, 0)
        product = lax.dot_general(matrix.astype(jnp.float32), sketch_block.astype(jnp.float32), (((0,), (0,)), ((), ())), preferred_element_type=jnp.float32)
        current = lax.dynamic_slice_in_dim(running, col_start, tile_size, 0)
        return lax.dynamic_update_slice_in_dim(running, current + product * live_mask, col_start, 0)
    column_sum = lax.fori_loop(0, tile_total, first_pass, jnp.zeros((COLS, sketch_width), jnp.float32))
    columns = column_sum.astype(jnp.bfloat16)

    def second_pass(position, running):
        matrix, live_mask, row_start, col_start = coords(position)
        column_block = lax.dynamic_slice_in_dim(columns, col_start, tile_size, 0)
        product = jnp.dot(matrix.astype(jnp.float32), column_block.astype(jnp.float32), preferred_element_type=jnp.float32)
        current = lax.dynamic_slice_in_dim(running, row_start, tile_size, 0)
        return lax.dynamic_update_slice_in_dim(running, current + product * live_mask, row_start, 0)
    new_sketch = lax.fori_loop(0, tile_total, second_pass, jnp.zeros((ROWS, sketch_width), jnp.float32))
    gram_matrix = jnp.dot(new_sketch.T.astype(jnp.float32), new_sketch.astype(jnp.float32), precision=lax.Precision.HIGHEST, preferred_element_type=jnp.float32) / ROWS
    cholesky_lower = jnp.linalg.cholesky(gram_matrix)
    basis_rows = lax.linalg.triangular_solve(cholesky_lower, new_sketch, left_side=False, lower=True, transpose_a=True)
    return (basis_rows, cholesky_lower.T)
```

```python
import jax
import jax.numpy as jnp
from jax import lax
from jax.experimental import pallas as pl
from jax.experimental.pallas import tpu as pltpu
from jax.sharding import PartitionSpec as P

BR = 12
BC = 12
GROUP = 16
VMEM_LIMIT = 52 * 1024 * 1024


def swap(value, axis, offset):
    size = lax.axis_size(axis)
    return lax.ppermute(value, axis, [(i, i ^ offset) for i in range(size)])


def fetch_tiles(count, tiles_ref, tile_buf, sems):
    slots = tiles_ref.shape[0]
    for slot in range(slots):
        @pl.when(slot < count)
        def _():
            pltpu.make_async_copy(tiles_ref.at[slot], tile_buf.at[slot], sems.at[slot]).start()


def wait_tile(slot, tiles_ref, tile_buf, sems):
    pltpu.make_async_copy(tiles_ref.at[slot], tile_buf.at[slot], sems.at[slot]).wait()


def transposed_kernel(count_ref, rows_ref, cols_ref, tiles_ref, *refs):
    pieces, (mine_ref, other_ref, sketch_buf, tile_buf, sems) = refs[:-5], refs[-5:]
    count = count_ref[0, 0]
    fetch_tiles(count, tiles_ref, tile_buf, sems)
    row_index, col_index = lax.axis_index("row"), lax.axis_index("col")
    tile_size = tiles_ref.shape[1]
    width = pieces[0].shape[1]
    groups = pieces[0].shape[0] // GROUP
    half = groups // 2
    core, place = row_index % 2, row_index // 2
    for offset, piece in enumerate(pieces):
        lanes = pl.ds(pl.multiple_of((col_index ^ offset) * width, 128), width)
        for group in range(groups):
            source = (core ^ (group // half)) * half + (place ^ (group % half))
            sketch_buf[pl.ds(group * GROUP, GROUP), lanes] = piece[
                pl.ds(pl.multiple_of(source * GROUP, GROUP), GROUP), :
            ]
    mine_ref[...] = jnp.zeros_like(mine_ref)
    other_ref[...] = jnp.zeros_like(other_ref)
    split = mine_ref.shape[0]

    def step(slot, carry):
        wait_tile(slot, tiles_ref, tile_buf, sems)
        block = sketch_buf[:, pl.ds(pl.multiple_of(rows_ref[0, 0, slot] * tile_size, 128), tile_size)]
        product = jnp.dot(block, tile_buf[slot], preferred_element_type=jnp.float32)
        lanes = pl.ds(pl.multiple_of(cols_ref[0, 0, slot] * tile_size, 128), tile_size)
        mine_ref[:, lanes] += product[:split]
        other_ref[:, lanes] += product[split:]
        return carry

    lax.fori_loop(0, count, step, 0)


def forward_kernel(count_ref, rows_ref, cols_ref, tiles_ref, *refs):
    pieces, (out_ref, column_buf, total, tile_buf, sems) = refs[:-5], refs[-5:]
    count = count_ref[0, 0]
    fetch_tiles(count, tiles_ref, tile_buf, sems)
    row_index, col_index = lax.axis_index("row"), lax.axis_index("col")
    tile_size = tiles_ref.shape[1]
    half = len(pieces) // 2
    core, place = row_index % 2, row_index // 2
    for offset, piece in enumerate(pieces):
        target = (core ^ (offset // half)) * half + (place ^ (offset % half))
        column_buf[pl.ds(pl.multiple_of(target * GROUP, GROUP), GROUP), :] = piece[...]
    total[...] = jnp.zeros_like(total)

    def step(slot, carry):
        wait_tile(slot, tiles_ref, tile_buf, sems)
        block = column_buf[:, pl.ds(pl.multiple_of(cols_ref[0, 0, slot] * tile_size, 128), tile_size)]
        product = lax.dot_general(
            tile_buf[slot], block, (((1,), (1,)), ((), ())), preferred_element_type=jnp.float32
        )
        total[pl.ds(pl.multiple_of(rows_ref[0, 0, slot] * tile_size, 128), tile_size), :] += product
        return carry

    lax.fori_loop(0, count, step, 0)
    width = out_ref.shape[1]
    for offset in range(out_ref.shape[0]):
        start = pl.multiple_of((col_index ^ offset) * width, 128)
        out_ref[offset] = total[pl.ds(start, width), :]


def tile_call(kernel, out_shape, scratch, counts, rows, cols, tiles, pieces):
    slots, tile_size, _ = tiles.shape
    smem = pl.BlockSpec(memory_space=pltpu.SMEM)
    vmem = pl.BlockSpec(memory_space=pltpu.VMEM)
    width = sum(p.shape[0] * p.shape[1] for p in pieces)
    return pl.pallas_call(
        kernel,
        out_shape=out_shape,
        in_specs=[smem, smem, smem, pl.BlockSpec(memory_space=pl.ANY)] + [vmem] * len(pieces),
        out_specs=jax.tree.map(lambda _: vmem, out_shape),
        scratch_shapes=scratch
        + [
            pltpu.VMEM((slots, tile_size, tile_size), jnp.bfloat16),
            pltpu.SemaphoreType.DMA((slots,)),
        ],
        compiler_params=pltpu.CompilerParams(vmem_limit_bytes=VMEM_LIMIT),
        cost_estimate=pl.CostEstimate(
            flops=2 * slots * tile_size * width // BR, bytes_accessed=2 * tiles.size, transcendentals=0
        ),
    )(counts, rows, cols, tiles, *pieces)


def gather_sketch(shard):
    return [shard] + [swap(shard, "col", d) for d in range(1, lax.axis_size("col"))]


def sum_columns(mine, other):
    places = lax.axis_size("row") // 2
    low = lambda d: d & -d
    arrived = swap(other.astype(jnp.float16), "row", 1)
    mine = mine + arrived.astype(jnp.float32)
    parts = {d: mine[d * GROUP : (d + 1) * GROUP] for d in range(places)}
    for d in range(places - 1, 0, -1):
        parts[d ^ low(d)] = parts[d ^ low(d)] + swap(
            parts[d].astype(jnp.float16), "row", 2 * low(d)
        ).astype(jnp.float32)
    whole = {0: parts[0].astype(jnp.bfloat16)}
    for d in sorted(range(1, places), key=lambda d: (bin(d).count("1"), -d)):
        whole[d] = swap(whole[d ^ low(d)], "row", 2 * low(d))
    near = [whole[d] for d in range(places)]
    return near + [swap(v, "row", 1) for v in near]


def sum_rows(parts):
    sent = parts[1:].astype(jnp.float16)
    total = parts[0]
    for d in range(1, parts.shape[0]):
        total = total + swap(sent[d - 1], "col", d).astype(jnp.float32)
    return total


def sum_everywhere(value):
    half = value.shape[0] // 2
    core = lax.axis_index("row") % 2
    mine = lax.dynamic_slice_in_dim(value, core * half, half, 0)
    other = lax.dynamic_slice_in_dim(value, (1 - core) * half, half, 0)
    mine = mine + swap(other, "row", 1)
    arrived = [swap(mine, "col", d) for d in range(1, lax.axis_size("col"))]
    stack = jnp.stack([mine] + arrived)
    mine = sum(
        lax.dynamic_index_in_dim(stack, lax.axis_index("col") ^ d, 0, keepdims=False)
        for d in range(lax.axis_size("col"))
    )
    bit = 2
    while bit < lax.axis_size("row"):
        mine = mine + swap(mine, "row", bit)
        bit *= 2
    other = swap(mine, "row", 1)
    return jnp.where(
        core == 0, jnp.concatenate([mine, other]), jnp.concatenate([other, mine])
    )


def body(tiles, tile_rows, tile_cols, tile_counts, sketch):
    tiles = tiles[0, 0]
    slots, tile_size, _ = tiles.shape
    width, sketch_width = sketch.shape
    chunk = min(sketch_width, GROUP * lax.axis_size("row"))
    group_rows, group_cols = BR * tile_size, BC * tile_size
    shard = sketch.T
    owned = []
    for start in range(0, sketch_width, chunk):
        pieces = gather_sketch(shard[start : start + chunk])
        half = jax.ShapeDtypeStruct((chunk // 2, group_cols), jnp.float32)
        mine, other = tile_call(
            transposed_kernel,
            (half, half),
            [pltpu.VMEM((chunk, group_rows), jnp.bfloat16)],
            tile_counts, tile_rows, tile_cols, tiles, pieces,
        )
        columns = sum_columns(mine, other)
        parts = tile_call(
            forward_kernel,
            jax.ShapeDtypeStruct((group_rows // width, width, chunk), jnp.float32),
            [pltpu.VMEM((chunk, group_cols), jnp.bfloat16), pltpu.VMEM((group_rows, chunk), jnp.float32)],
            tile_counts, tile_rows, tile_cols, tiles, columns,
        )
        owned.append(sum_rows(parts))
    owned_rows = jnp.concatenate(owned, axis=1)
    total_rows = group_rows * lax.axis_size("row")
    local_gram = jnp.dot(
        owned_rows.T, owned_rows, precision=lax.Precision.HIGHEST, preferred_element_type=jnp.float32
    )
    gram_matrix = sum_everywhere(local_gram) / total_rows
    cholesky_lower = jnp.linalg.cholesky(gram_matrix)
    basis_rows = lax.linalg.triangular_solve(
        cholesky_lower, owned_rows, left_side=False, lower=True, transpose_a=True
    )
    return (basis_rows, cholesky_lower.T)


def solution(mesh):
    return jax.shard_map(
        body,
        mesh=mesh,
        in_specs=(
            P("row", "col", None, None, None),
            P("row", "col", None),
            P("row", "col", None),
            P("row", "col"),
            P(("row", "col"), None),
        ),
        out_specs=(P(("row", "col"), None), P()),
        check_vma=False,
    )
```

```python
import functools
import jax
import jax.numpy as jnp
from jax import lax
from jax.experimental import pallas as pl
from jax.experimental.pallas import tpu as pltpu
from jax.sharding import PartitionSpec as P

BR = 12
BC = 12
GROUP = 16
SUBLANES = 8
VMEM_LIMIT = 52 * 1024 * 1024
NO_COST = pl.CostEstimate(flops=0, bytes_accessed=0, transcendentals=0)


def swap(value, axis, offset):
    size = lax.axis_size(axis)
    return lax.ppermute(value, axis, [(i, i ^ offset) for i in range(size)])


def fetch_tiles(count, tiles_ref, tile_buf, sems):
    slots = tiles_ref.shape[0]
    for slot in range(slots):
        @pl.when(slot < count)
        def _():
            pltpu.make_async_copy(tiles_ref.at[slot], tile_buf.at[slot], sems.at[slot]).start()


def wait_tile(slot, tiles_ref, tile_buf, sems):
    pltpu.make_async_copy(tiles_ref.at[slot], tile_buf.at[slot], sems.at[slot]).wait()


def transposed_kernel(count_ref, rows_ref, cols_ref, tiles_ref, *refs):
    pieces, (mine_ref, other_ref, sketch_buf, tile_buf, sems) = refs[:-5], refs[-5:]
    count = count_ref[0, 0]
    fetch_tiles(count, tiles_ref, tile_buf, sems)
    row_index, col_index = lax.axis_index("row"), lax.axis_index("col")
    tile_size = tiles_ref.shape[1]
    width = pieces[0].shape[1]
    groups = pieces[0].shape[0] // GROUP
    half = groups // 2
    core, place = row_index % 2, row_index // 2
    for offset, piece in enumerate(pieces):
        lanes = pl.ds(pl.multiple_of((col_index ^ offset) * width, 128), width)
        for group in range(groups):
            source = (core ^ (group // half)) * half + (place ^ (group % half))
            sketch_buf[pl.ds(group * GROUP, GROUP), lanes] = piece[
                pl.ds(pl.multiple_of(source * GROUP, GROUP), GROUP), :
            ]
    mine_ref[...] = jnp.zeros_like(mine_ref)
    other_ref[...] = jnp.zeros_like(other_ref)
    split = mine_ref.shape[0]

    def step(slot, carry):
        wait_tile(slot, tiles_ref, tile_buf, sems)
        block = sketch_buf[:, pl.ds(pl.multiple_of(rows_ref[0, 0, slot] * tile_size, 128), tile_size)]
        product = jnp.dot(block, tile_buf[slot], preferred_element_type=jnp.float32)
        lanes = pl.ds(pl.multiple_of(cols_ref[0, 0, slot] * tile_size, 128), tile_size)
        mine_ref[:, lanes] += product[:split]
        other_ref[:, lanes] += product[split:]
        return carry

    lax.fori_loop(0, count, step, 0)


def forward_kernel(count_ref, rows_ref, cols_ref, tiles_ref, *refs):
    outs = lax.axis_size("col")
    column_buf, total, tile_buf, sems = refs[-4:]
    pieces, out_refs = refs[: -4 - outs], refs[-4 - outs : -4]
    count = count_ref[0, 0]
    fetch_tiles(count, tiles_ref, tile_buf, sems)
    row_index, col_index = lax.axis_index("row"), lax.axis_index("col")
    tile_size = tiles_ref.shape[1]
    half = len(pieces) // 2
    core, place = row_index % 2, row_index // 2
    for offset, piece in enumerate(pieces):
        target = (core ^ (offset // half)) * half + (place ^ (offset % half))
        column_buf[pl.ds(pl.multiple_of(target * GROUP, GROUP), GROUP), :] = piece[...]
    total[...] = jnp.zeros_like(total)

    def step(slot, carry):
        wait_tile(slot, tiles_ref, tile_buf, sems)
        block = column_buf[:, pl.ds(pl.multiple_of(cols_ref[0, 0, slot] * tile_size, 128), tile_size)]
        product = lax.dot_general(
            tile_buf[slot], block, (((1,), (1,)), ((), ())), preferred_element_type=jnp.float32
        )
        total[pl.ds(pl.multiple_of(rows_ref[0, 0, slot] * tile_size, 128), tile_size), :] += product
        return carry

    lax.fori_loop(0, count, step, 0)
    for offset, out_ref in enumerate(out_refs):
        width = out_ref.shape[0]
        start = pl.multiple_of((col_index ^ offset) * width, 128)
        out_ref[...] = total[pl.ds(start, width), :].astype(out_ref.dtype)


def tile_call(kernel, out_shape, scratch, counts, rows, cols, tiles, pieces):
    slots, tile_size, _ = tiles.shape
    smem = pl.BlockSpec(memory_space=pltpu.SMEM)
    vmem = pl.BlockSpec(memory_space=pltpu.VMEM)
    return pl.pallas_call(
        kernel,
        out_shape=out_shape,
        in_specs=[smem, smem, smem, pl.BlockSpec(memory_space=pl.ANY)] + [vmem] * len(pieces),
        out_specs=jax.tree.map(lambda _: vmem, out_shape),
        scratch_shapes=scratch
        + [
            pltpu.VMEM((slots, tile_size, tile_size), jnp.bfloat16),
            pltpu.SemaphoreType.DMA((slots,)),
        ],
        compiler_params=pltpu.CompilerParams(vmem_limit_bytes=VMEM_LIMIT),
        cost_estimate=NO_COST,
    )(counts, rows, cols, tiles, *pieces)


def after(value, token):
    return value if token is None else lax.optimization_barrier((value, token))[0]


def half(value):
    return value.astype(jnp.float16)


def full(value):
    return value.astype(jnp.float32)


class Chunk:
    def __init__(self, call_transposed, call_forward, shard):
        self.call_transposed, self.call_forward = call_transposed, call_forward
        self.places = lax.axis_size("row") // 2
        self.offsets = range(1, lax.axis_size("col"))
        self.low = lambda d: d & -d
        self.pieces = [shard] + [swap(shard, "col", d) for d in self.offsets]

    def multiply_transposed(self, token=None):
        self.mine, self.other = self.call_transposed(after(self.pieces, token))

    def send_other(self, token=None):
        self.sent = after(self.other, token)
        self.arrived = swap(self.sent, "row", 1)

    def reduce_begin(self, token=None):
        arrived = after(self.arrived, token)
        rows = lambda value, d: value[d * GROUP : (d + 1) * GROUP]
        self.parts = {d: rows(self.mine, d) + rows(arrived, d) for d in range(self.places)}
        self.arriving = {d: [] for d in range(self.places)}
        for d in range(3, self.places, 2):
            self.pass_on(d)

    def pass_on(self, d, token=None):
        for value in after(self.arriving[d], token):
            self.parts[d] = self.parts[d] + full(value)
        self.sent = half(self.parts[d])
        bit = self.low(d)
        self.arriving[d ^ bit].append(swap(self.sent, "row", 2 * bit))

    def reduce_rest(self, token=None):
        for d in sorted(range(2, self.places, 2), key=lambda d: (self.low(d), d)):
            self.pass_on(d, token)
            token = None
        self.parts[1] = after(self.parts[1], self.sent)
        self.pass_on(1)

    def own(self, token=None):
        for value in after(self.arriving[0], token):
            self.parts[0] = self.parts[0] + full(value)
        self.whole = {0: self.parts[0].astype(jnp.bfloat16)}
        self.ways = sorted(range(1, self.places), key=lambda d: (bin(d).count("1"), -d))
        for d in self.ways:
            if bin(d).count("1") == 1 and d > 1:
                self.spread(d)

    def spread(self, d, token=None):
        self.whole[d] = swap(after(self.whole[d ^ self.low(d)], token), "row", 2 * self.low(d))

    def spread_rest(self, token=None):
        first = self.ways[0]
        if token is not None:
            self.whole[first] = after(self.whole[first], token)
        for d in self.ways:
            if d not in self.whole:
                self.spread(d)

    def share(self, token=None):
        near = [self.whole[d] for d in range(self.places)]
        late = [d for d in range(1, self.places) if d != self.ways[0]]
        for d, value in zip(late, after([near[d] for d in late], token)):
            near[d] = value
        self.columns = near + [swap(v, "row", 1) for v in near]

    def multiply_forward(self, token=None):
        self.forward = self.call_forward(after(self.columns, token))

    def send_rows(self, token=None):
        self.total, *self.sent = after(self.forward, token)
        self.arrived = [swap(value, "col", d) for d, value in zip(self.offsets, self.sent)]

    def finish(self, token=None, *others):
        parts = [self.total] + after(self.arrived, token)
        shape = self.total.shape
        return pl.pallas_call(
            finish_kernel,
            out_shape=(
                jax.ShapeDtypeStruct(shape, jnp.float32),
                jax.ShapeDtypeStruct((shape[1] * (len(others) + 1), shape[1]), jnp.float32),
            ),
            compiler_params=pltpu.CompilerParams(vmem_limit_bytes=VMEM_LIMIT),
            cost_estimate=NO_COST,
        )(*others, *parts)


def run_alone(chunk):
    for step in (
        chunk.multiply_transposed, chunk.send_other, chunk.reduce_begin, chunk.reduce_rest, chunk.own,
        chunk.spread_rest, chunk.share, chunk.multiply_forward, chunk.send_rows,
    ):
        step()
    return chunk.finish()


def run_pair(a, b):
    a.multiply_transposed()
    a.send_other(b.pieces[1:3])
    a.reduce_begin()
    a.reduce_rest()
    b.multiply_transposed(a.sent)
    b.send_other(a.arriving[0])
    a.own(b.sent)
    a.spread(1)
    b.reduce_begin(a.whole[0])
    a.spread_rest(b.sent)
    b.reduce_rest([a.whole[1], a.whole[2]])
    b.own()
    b.spread(1)
    a.share(b.whole[0])
    a.multiply_forward()
    a.send_rows(b.whole[1])
    b.spread_rest(a.sent)
    b.share()
    b.multiply_forward(a.sent)
    b.send_rows()


class Sum:
    def __init__(self, value):
        half = value.shape[0] // 2
        self.core = lax.axis_index("row") % 2
        mine = lax.dynamic_slice_in_dim(value, self.core * half, half, 0)
        other = lax.dynamic_slice_in_dim(value, (1 - self.core) * half, half, 0)
        self.mine = mine + swap(other, "row", 1)

    def over_row(self, token=None):
        bit = 2
        while bit < lax.axis_size("row"):
            arrived = swap(self.mine, "row", bit)
            if token is not None and bit == 2:
                arrived = after(arrived, token)
            self.mine = self.mine + arrived
            bit *= 2

    def over_col(self, token=None):
        mine = after(self.mine, token)
        arrived = [swap(mine, "col", d) for d in range(1, lax.axis_size("col"))]
        stack = jnp.stack([mine] + arrived)
        self.mine = sum(
            lax.dynamic_index_in_dim(stack, lax.axis_index("col") ^ d, 0, keepdims=False)
            for d in range(lax.axis_size("col"))
        )

    def finish(self):
        other = swap(self.mine, "row", 1)
        return jnp.where(
            self.core == 0, jnp.concatenate([self.mine, other]), jnp.concatenate([other, self.mine])
        )


def product(left, right, left_dim, right_dim):
    return lax.dot_general(
        left, right, (((left_dim,), (right_dim,)), ((), ())),
        precision=lax.Precision.HIGHEST, preferred_element_type=jnp.float32,
    )


def finish_kernel(*refs):
    parts = lax.axis_size("col")
    rows_ref, gram_ref = refs[-2:]
    others, parts = refs[: -2 - parts], refs[-2 - parts : -2]
    total = parts[0][...]
    for part in parts[1:]:
        total = total + part[...].astype(jnp.float32)
    rows_ref[...] = total
    size = total.shape[1]
    for i, other in enumerate(others):
        gram_ref[size * i : size * (i + 1), :] = product(other[...], total, 0, 0)
    gram_ref[size * len(others) :, :] = product(total, total, 0, 0)


def factor_with_inverse(matrix):
    size = matrix.shape[1]
    groups = size // SUBLANES
    shape = (SUBLANES, size)
    row = lax.broadcasted_iota(jnp.int32, shape, 0)
    col = lax.broadcasted_iota(jnp.int32, shape, 1)
    left = [matrix[SUBLANES * g : SUBLANES * (g + 1), :] for g in range(groups)]
    right = [(col == row + SUBLANES * g).astype(jnp.float32) for g in range(groups)]
    spread = lambda value, j: jnp.broadcast_to(value[j : j + 1, :], shape)
    for p in range(groups):
        columns = [
            {
                g: jnp.broadcast_to(left[g][:, SUBLANES * p + k : SUBLANES * p + k + 1], shape)
                for g in range(p, groups)
            }
            for k in range(SUBLANES)
        ]
        pivots = None
        for j in range(SUBLANES):
            pivot = spread(columns[j][p], j)
            inverse = 1.0 / pivot
            pivots = pivot if pivots is None else jnp.where(row == j, pivot, pivots)
            left_row, right_row = spread(left[p], j), spread(right[p], j)
            heads = {k: spread(columns[k][p], j) for k in range(j + 1, SUBLANES)}
            for g in range(p, groups):
                scale = columns[j][g] * inverse
                if g == p:
                    scale = jnp.where(row > j, scale, 0.0)
                left[g] = left[g] - scale * left_row
                right[g] = right[g] - scale * right_row
                for k, head in heads.items():
                    columns[k][g] = columns[k][g] - scale * head
        scale = lax.rsqrt(pivots)
        left[p] = jnp.where(col >= row + SUBLANES * p, left[p] * scale, 0.0)
        right[p] = right[p] * scale
    return jnp.concatenate(left), jnp.concatenate(right)


def first_factor_kernel(total_rows, gram_ref, rows_ref, upper_ref, inverse_ref, basis_ref):
    upper, inverse = factor_with_inverse(gram_ref[...] / total_rows)
    upper_ref[...] = upper
    inverse_ref[...] = inverse
    basis_ref[...] = product(rows_ref[...], inverse, 1, 1)


def second_factor_kernel(
    total_rows, gram_ref, upper_ref, inverse_ref, first_ref, rows_ref, basis_ref, factor_ref
):
    split = upper_ref.shape[0]
    mixed, last = gram_ref[:split] / total_rows, gram_ref[split:] / total_rows
    corner = product(inverse_ref[...], mixed, 1, 0)
    upper, inverse = factor_with_inverse(last - product(corner, corner, 0, 0))
    factor_ref[:split, :split] = upper_ref[...]
    factor_ref[:split, split:] = corner
    factor_ref[split:, :split] = jnp.zeros_like(upper)
    factor_ref[split:, split:] = upper
    first = first_ref[...]
    basis_ref[:, :split] = first
    basis_ref[:, split:] = product(rows_ref[...], inverse, 1, 1) - product(
        first, product(corner, inverse, 1, 1), 1, 0
    )


def body(tiles, tile_rows, tile_cols, tile_counts, sketch):
    tiles = tiles[0, 0]
    slots, tile_size, _ = tiles.shape
    width, sketch_width = sketch.shape
    chunk = min(sketch_width, GROUP * lax.axis_size("row"))
    group_rows, group_cols = BR * tile_size, BC * tile_size
    shard = sketch.T
    partial = jax.ShapeDtypeStruct((chunk // 2, group_cols), jnp.float32)
    call_transposed = lambda pieces: tile_call(
        transposed_kernel,
        (partial, partial),
        [pltpu.VMEM((chunk, group_rows), jnp.bfloat16)],
        tile_counts, tile_rows, tile_cols, tiles, pieces,
    )
    call_forward = lambda pieces: tile_call(
        forward_kernel,
        tuple(
            jax.ShapeDtypeStruct((width, chunk), jnp.bfloat16 if offset else jnp.float32)
            for offset in range(lax.axis_size("col"))
        ),
        [pltpu.VMEM((chunk, group_cols), jnp.bfloat16), pltpu.VMEM((group_rows, chunk), jnp.float32)],
        tile_counts, tile_rows, tile_cols, tiles, pieces,
    )
    chunks = [
        Chunk(call_transposed, call_forward, shard[start : start + chunk])
        for start in range(0, sketch_width, chunk)
    ]
    split = sketch_width // 2
    if len(chunks) == 2:
        run_pair(*chunks)
        first, first_gram = chunks[0].finish(chunks[1].sent)
        first_gram = after(first_gram, chunks[1].arrived[:1])
    else:
        whole, gram = run_alone(chunks[0])
        first, second = whole[:, :split], whole[:, split:]
        first_gram, mixed_gram = gram[:split, :split], gram[:, split:]
    total_rows = group_rows * lax.axis_size("row")
    params = pltpu.CompilerParams(vmem_limit_bytes=VMEM_LIMIT)
    square = jax.ShapeDtypeStruct((split, split), jnp.float32)
    first_gram = Sum(first_gram)
    first_gram.over_row()
    if len(chunks) == 2:
        second, mixed_gram = chunks[1].finish(first_gram.mine, first)
    first_gram.over_col()
    mixed_gram = Sum(mixed_gram)
    upper, inverse, first_basis = pl.pallas_call(
        functools.partial(first_factor_kernel, total_rows),
        out_shape=(square, square, jax.ShapeDtypeStruct(first.shape, jnp.float32)),
        compiler_params=params,
    )(first_gram.finish(), first)
    mixed_gram.over_row(upper)
    mixed_gram.over_col()
    return pl.pallas_call(
        functools.partial(second_factor_kernel, total_rows),
        out_shape=(
            jax.ShapeDtypeStruct((width, sketch_width), jnp.float32),
            jax.ShapeDtypeStruct((sketch_width, sketch_width), jnp.float32),
        ),
        compiler_params=params,
    )(mixed_gram.finish(), upper, inverse, first_basis, second)


def solution(mesh):
    return jax.shard_map(
        body,
        mesh=mesh,
        in_specs=(
            P("row", "col", None, None, None),
            P("row", "col", None),
            P("row", "col", None),
            P("row", "col"),
            P(("row", "col"), None),
        ),
        out_specs=(P(("row", "col"), None), P()),
        check_vma=False,
    )
```

```python
import functools
import jax
import jax.numpy as jnp
from jax import lax
from jax.experimental import pallas as pl
from jax.experimental.pallas import tpu as pltpu
from jax.sharding import PartitionSpec as P

BR = 12
BC = 12
GROUP = 16
SUBLANES = 8
VMEM_LIMIT = 52 * 1024 * 1024
NO_COST = pl.CostEstimate(flops=0, bytes_accessed=0, transcendentals=0)


def swap(value, axis, offset):
    size = lax.axis_size(axis)
    return lax.ppermute(value, axis, [(i, i ^ offset) for i in range(size)])


def fetch_tiles(count, tiles_ref, tile_buf, sems):
    slots = tiles_ref.shape[0]
    for slot in range(slots):
        @pl.when(slot < count)
        def _():
            pltpu.make_async_copy(tiles_ref.at[slot], tile_buf.at[slot], sems.at[slot]).start()


def wait_tile(slot, tiles_ref, tile_buf, sems):
    pltpu.make_async_copy(tiles_ref.at[slot], tile_buf.at[slot], sems.at[slot]).wait()


def prepare_kernel(sketch_ref, *refs):
    urgent_ref, *half_refs, flipped = refs
    row_index = lax.axis_index("row")
    core, place = row_index % 2, row_index // 2
    places = lax.axis_size("row") // 2
    flipped[...] = sketch_ref[...].T

    def copy(target, index, half, which_core, offset):
        group = (half * 2 + (core ^ which_core)) * places + (place ^ offset)
        target[GROUP * index : GROUP * (index + 1), :] = flipped[
            pl.ds(pl.multiple_of(group * GROUP, GROUP), GROUP), :
        ]

    for which_core in range(2):
        for half, half_ref in enumerate(half_refs):
            copy(urgent_ref, which_core * len(half_refs) + half, half, which_core, places - 1)
            for offset in range(places - 1):
                copy(half_ref, which_core * (places - 1) + offset, half, which_core, offset)


def transposed_kernel(places, count_ref, rows_ref, cols_ref, tiles_ref, *refs):
    *out_refs, sketch_buf, tile_buf, sems = refs[len(places) :]
    count = count_ref[0, 0]
    fetch_tiles(count, tiles_ref, tile_buf, sems)
    col_index = lax.axis_index("col")
    tile_size = tiles_ref.shape[1]
    for (offset, start), piece in zip(places, refs):
        depth, width = piece.shape
        lanes = pl.ds(pl.multiple_of((col_index ^ offset) * width, 128), width)
        if width == sketch_buf.shape[1]:
            lanes = slice(None)
        sketch_buf[start : start + depth, lanes] = piece[...]
    for out_ref in out_refs:
        out_ref[...] = jnp.zeros_like(out_ref)

    def step(slot, carry):
        wait_tile(slot, tiles_ref, tile_buf, sems)
        block = sketch_buf[:, pl.ds(pl.multiple_of(rows_ref[0, 0, slot] * tile_size, 128), tile_size)]
        product = jnp.dot(block, tile_buf[slot], preferred_element_type=jnp.float32)
        lanes = pl.ds(pl.multiple_of(cols_ref[0, 0, slot] * tile_size, 128), tile_size)
        depth = out_refs[0].shape[0]
        for i, out_ref in enumerate(out_refs):
            out_ref[:, lanes] += product[depth * i : depth * (i + 1)]
        return carry

    lax.fori_loop(0, count, step, 0)


def forward_kernel(outs, count_ref, rows_ref, cols_ref, tiles_ref, *refs):
    column_buf, total, tile_buf, sems = refs[-4:]
    pieces, out_refs = refs[: -4 - outs], refs[-4 - outs : -4]
    count = count_ref[0, 0]
    fetch_tiles(count, tiles_ref, tile_buf, sems)
    row_index, col_index = lax.axis_index("row"), lax.axis_index("col")
    tile_size = tiles_ref.shape[1]
    half = len(pieces) // 2
    core, place = row_index % 2, row_index // 2
    for offset, piece in enumerate(pieces):
        if half:
            target = (core ^ (offset // half)) * half + (place ^ (offset % half))
            column_buf[pl.ds(pl.multiple_of(target * GROUP, GROUP), GROUP), :] = piece[...]
        else:
            column_buf[...] = piece[...]
    total[...] = jnp.zeros_like(total)

    def step(slot, carry):
        wait_tile(slot, tiles_ref, tile_buf, sems)
        block = column_buf[:, pl.ds(pl.multiple_of(cols_ref[0, 0, slot] * tile_size, 128), tile_size)]
        product = lax.dot_general(
            tile_buf[slot], block, (((1,), (1,)), ((), ())), preferred_element_type=jnp.float32
        )
        total[pl.ds(pl.multiple_of(rows_ref[0, 0, slot] * tile_size, 128), tile_size), :] += product
        return carry

    lax.fori_loop(0, count, step, 0)
    for offset, out_ref in enumerate(out_refs):
        width = out_ref.shape[0]
        if outs == 1:
            out_ref[...] = total[...]
        else:
            start = pl.multiple_of((col_index ^ offset) * width, 128)
            out_ref[...] = total[pl.ds(start, width), :].astype(out_ref.dtype)


def tile_call(kernel, out_shape, scratch, counts, rows, cols, tiles, pieces):
    slots, tile_size, _ = tiles.shape
    smem = pl.BlockSpec(memory_space=pltpu.SMEM)
    vmem = pl.BlockSpec(memory_space=pltpu.VMEM)
    return pl.pallas_call(
        kernel,
        out_shape=out_shape,
        in_specs=[smem, smem, smem, pl.BlockSpec(memory_space=pl.ANY)] + [vmem] * len(pieces),
        out_specs=jax.tree.map(lambda _: vmem, out_shape),
        scratch_shapes=scratch
        + [
            pltpu.VMEM((slots, tile_size, tile_size), jnp.bfloat16),
            pltpu.SemaphoreType.DMA((slots,)),
        ],
        compiler_params=pltpu.CompilerParams(vmem_limit_bytes=VMEM_LIMIT),
        cost_estimate=NO_COST,
    )(counts, rows, cols, tiles, *pieces)


def after(value, token):
    return value if token is None else lax.optimization_barrier((value, token))[0]


def half(value):
    return value.astype(jnp.float16)


def full(value):
    return value.astype(jnp.float32)


def gather(shard):
    return [(0, 0, shard)] + [(d, 0, swap(shard, "col", d)) for d in range(1, lax.axis_size("col"))]


class Half:
    def __init__(self, call_transposed, call_forward, shard):
        self.call_transposed, self.call_forward = call_transposed, call_forward
        self.shard = shard

    def gather_near(self):
        self.middle = self.shard.shape[0] // 2
        parts = [self.shard[: self.middle], self.shard[self.middle :]]
        self.near = [[swap(part, "col", d) for part in parts] for d in (1, 2)]

    def gather_far(self):
        first, second = self.near
        self.pieces = [(0, 0, self.shard)]
        self.pieces += [(d, self.middle * i, part) for d in (1, 2) for i, part in enumerate(self.near[d - 1])]
        self.pieces.append((3, 0, swap(second[0], "col", 1)))
        self.pieces.append((3, self.middle, swap(first[1], "col", 2)))

    def multiply_transposed(self, token=None):
        self.mine, self.other = self.call_transposed(self.pieces, token)

    def send_other(self, token=None):
        self.arrived = swap(after(self.other, token), "row", 1)

    def reduce(self, far):
        rows = lambda value, d: value[d * GROUP : (d + 1) * GROUP]
        self.parts = [rows(self.mine, d) + rows(self.arrived, d) for d in range(3)]
        self.sent = half(self.parts[2] + full(far))
        middle = swap(self.sent, "row", 4)
        self.arriving = [middle]

    def reduce_last(self, token):
        self.arriving.append(swap(half(after(self.parts[1], token)), "row", 2))

    def own(self, token=None):
        middle, low = after(self.arriving, token)
        self.whole = {0: (self.parts[0] + full(middle) + full(low)).astype(jnp.bfloat16)}
        self.whole[2] = swap(self.whole[0], "row", 4)
        self.whole[1] = swap(self.whole[0], "row", 2)

    def spread(self, token=None):
        self.whole[2] = after(self.whole[2], token)
        self.whole[3] = swap(self.whole[2], "row", 2)

    def share(self, token=None):
        self.whole[1], self.whole[3] = after([self.whole[1], self.whole[3]], token)
        near = [self.whole[d] for d in range(4)]
        self.columns = near + [swap(v, "row", 1) for v in near]

    def multiply_forward(self, token=None):
        self.forward = self.call_forward(after(self.columns, token))

    def send_rows(self, token=None):
        self.total, *self.sent = after(self.forward, token)
        self.arrived = [swap(value, "col", d + 1) for d, value in enumerate(self.sent)]

    def finish(self, token=None, *others):
        return finish_call([self.total] + after(self.arrived, token), *others)


def finish_call(parts, *others):
    shape = parts[0].shape
    return pl.pallas_call(
        functools.partial(finish_kernel, len(parts)),
        out_shape=(
            jax.ShapeDtypeStruct(shape, jnp.float32),
            jax.ShapeDtypeStruct((shape[1] * (len(others) + 1), shape[1]), jnp.float32),
        ),
        compiler_params=pltpu.CompilerParams(vmem_limit_bytes=VMEM_LIMIT),
        cost_estimate=NO_COST,
    )(*others, *parts)


def run_pair(call_transposed, a, b, urgent):
    pieces = gather(urgent)
    a.gather_near()
    mine, other = call_transposed(pieces, None)
    arrived = swap(after(other, a.near), "row", 1)
    a.gather_far()
    b.shard = after(b.shard, [piece[2] for piece in a.pieces[5:]])
    b.gather_near()
    sent = half(mine + arrived)
    far = swap(sent, "row", 2)
    a.multiply_transposed(sent)
    a.send_other([b.near, far])
    b.gather_far()
    a.reduce(far[:GROUP])
    a.reduce_last(a.sent)
    b.multiply_transposed(a.sent)
    b.send_other(a.arriving[0])
    a.own(b.other)
    b.reduce(after(far[GROUP:], a.whole[0]))
    a.spread(b.sent)
    b.reduce_last(a.whole[3])
    a.share()
    a.multiply_forward()
    b.own(a.forward)
    a.send_rows()
    b.spread(a.arrived[:2])
    b.share()
    b.multiply_forward()
    b.send_rows(a.arrived[2:])


class Sum:
    def __init__(self, value):
        half = value.shape[0] // 2
        self.core = lax.axis_index("row") % 2
        mine = lax.dynamic_slice_in_dim(value, self.core * half, half, 0)
        other = lax.dynamic_slice_in_dim(value, (1 - self.core) * half, half, 0)
        self.mine = mine + swap(other, "row", 1)

    def over_row(self, tokens):
        bit = 2
        while bit < lax.axis_size("row"):
            self.mine = self.mine + after(swap(self.mine, "row", bit), tokens.get(bit))
            bit *= 2

    def over_col(self, token=None):
        mine = after(self.mine, token)
        arrived = [swap(mine, "col", d) for d in range(1, lax.axis_size("col"))]
        stack = jnp.stack([mine] + arrived)
        self.mine = sum(
            lax.dynamic_index_in_dim(stack, lax.axis_index("col") ^ d, 0, keepdims=False)
            for d in range(lax.axis_size("col"))
        )

    def finish(self):
        other = swap(self.mine, "row", 1)
        return jnp.where(
            self.core == 0, jnp.concatenate([self.mine, other]), jnp.concatenate([other, self.mine])
        )


def product(left, right, left_dim, right_dim):
    return lax.dot_general(
        left, right, (((left_dim,), (right_dim,)), ((), ())),
        precision=lax.Precision.HIGHEST, preferred_element_type=jnp.float32,
    )


def finish_kernel(parts, *refs):
    rows_ref, gram_ref = refs[-2:]
    others, parts = refs[: -2 - parts], refs[-2 - parts : -2]
    total = parts[0][...]
    for part in parts[1:]:
        total = total + part[...].astype(jnp.float32)
    rows_ref[...] = total
    size = total.shape[1]
    for i, other in enumerate(others):
        gram_ref[size * i : size * (i + 1), :] = product(other[...], total, 0, 0)
    gram_ref[size * len(others) :, :] = product(total, total, 0, 0)


def factor_with_inverse(matrix):
    size = matrix.shape[1]
    groups = size // SUBLANES
    shape = (SUBLANES, size)
    row = lax.broadcasted_iota(jnp.int32, shape, 0)
    col = lax.broadcasted_iota(jnp.int32, shape, 1)
    left = [matrix[SUBLANES * g : SUBLANES * (g + 1), :] for g in range(groups)]
    right = [(col == row + SUBLANES * g).astype(jnp.float32) for g in range(groups)]
    spread = lambda value, j: jnp.broadcast_to(value[j : j + 1, :], shape)
    for p in range(groups):
        columns = [
            {
                g: jnp.broadcast_to(left[g][:, SUBLANES * p + k : SUBLANES * p + k + 1], shape)
                for g in range(p, groups)
            }
            for k in range(SUBLANES)
        ]
        pivots = None
        for j in range(SUBLANES):
            pivot = spread(columns[j][p], j)
            inverse = 1.0 / pivot
            pivots = pivot if pivots is None else jnp.where(row == j, pivot, pivots)
            left_row, right_row = spread(left[p], j), spread(right[p], j)
            heads = {k: spread(columns[k][p], j) for k in range(j + 1, SUBLANES)}
            for g in range(p, groups):
                scale = columns[j][g] * inverse
                if g == p:
                    scale = jnp.where(row > j, scale, 0.0)
                left[g] = left[g] - scale * left_row
                right[g] = right[g] - scale * right_row
                for k, head in heads.items():
                    columns[k][g] = columns[k][g] - scale * head
        scale = lax.rsqrt(pivots)
        left[p] = jnp.where(col >= row + SUBLANES * p, left[p] * scale, 0.0)
        right[p] = right[p] * scale
    return jnp.concatenate(left), jnp.concatenate(right)


def first_factor_kernel(total_rows, gram_ref, rows_ref, upper_ref, inverse_ref, basis_ref):
    upper, inverse = factor_with_inverse(gram_ref[...] / total_rows)
    upper_ref[...] = upper
    inverse_ref[...] = inverse
    basis_ref[...] = product(rows_ref[...], inverse, 1, 1)


def second_factor_kernel(
    total_rows, gram_ref, upper_ref, inverse_ref, first_ref, rows_ref, basis_ref, factor_ref
):
    split = upper_ref.shape[0]
    mixed, last = gram_ref[:split] / total_rows, gram_ref[split:] / total_rows
    corner = product(inverse_ref[...], mixed, 1, 0)
    upper, inverse = factor_with_inverse(last - product(corner, corner, 0, 0))
    factor_ref[:split, :split] = upper_ref[...]
    factor_ref[:split, split:] = corner
    factor_ref[split:, :split] = jnp.zeros_like(upper)
    factor_ref[split:, split:] = upper
    first = first_ref[...]
    basis_ref[:, :split] = first
    basis_ref[:, split:] = product(rows_ref[...], inverse, 1, 1) - product(
        first, product(corner, inverse, 1, 1), 1, 0
    )


def body(tiles, tile_rows, tile_cols, tile_counts, sketch):
    tiles = tiles[0, 0]
    slots, tile_size, _ = tiles.shape
    width, sketch_width = sketch.shape
    group_rows, group_cols = BR * tile_size, BC * tile_size
    split = sketch_width // 2
    rows_axis, cols_axis = lax.axis_size("row"), lax.axis_size("col")

    def call_transposed(pieces, token):
        depth = pieces[0][2].shape[0]
        outs = 2 if rows_axis == 8 else 1
        return tile_call(
            functools.partial(transposed_kernel, [piece[:2] for piece in pieces]),
            [jax.ShapeDtypeStruct((depth // outs, group_cols), jnp.float32)] * outs,
            [pltpu.VMEM((depth, group_rows), jnp.bfloat16)],
            tile_counts, tile_rows, tile_cols, tiles, after([piece[2] for piece in pieces], token),
        )

    def call_forward(columns, outs=cols_axis):
        depth = sum(piece.shape[0] for piece in columns)
        return tile_call(
            functools.partial(forward_kernel, outs),
            [
                jax.ShapeDtypeStruct((group_rows // outs, depth), jnp.bfloat16 if offset else jnp.float32)
                for offset in range(outs)
            ],
            [pltpu.VMEM((depth, group_cols), jnp.bfloat16), pltpu.VMEM((group_rows, depth), jnp.float32)],
            tile_counts, tile_rows, tile_cols, tiles, columns,
        )

    paired = rows_axis == 8 and cols_axis == 4 and sketch_width == 2 * GROUP * rows_axis
    if paired:
        part = lambda groups: jax.ShapeDtypeStruct((groups * GROUP, width), jnp.bfloat16)
        urgent, *halves = pl.pallas_call(
            prepare_kernel,
            out_shape=[part(4), part(6), part(6)],
            scratch_shapes=[pltpu.VMEM((sketch_width, width), jnp.bfloat16)],
            compiler_params=pltpu.CompilerParams(vmem_limit_bytes=VMEM_LIMIT),
            cost_estimate=NO_COST,
        )(sketch)
        a, b = [Half(call_transposed, call_forward, shard) for shard in halves]
        run_pair(call_transposed, a, b, urgent)
        first, first_gram = a.finish(b.sent)
    else:
        everything = lax.all_gather(sketch.T, "col", axis=1, tiled=True)
        (partial,) = call_transposed([(0, 0, everything)], None)
        columns = lax.psum_scatter(partial, "row", scatter_dimension=0, tiled=True).astype(jnp.bfloat16)
        columns = lax.all_gather(columns, "row", axis=0, tiled=True)
        (partial,) = call_forward([columns], 1)
        whole, gram = finish_call([lax.psum_scatter(partial, "col", scatter_dimension=0, tiled=True)])
        first, second = whole[:, :split], whole[:, split:]
        first_gram, mixed_gram = gram[:split, :split], gram[:, split:]
    total_rows = group_rows * lax.axis_size("row")
    params = pltpu.CompilerParams(vmem_limit_bytes=VMEM_LIMIT)
    square = jax.ShapeDtypeStruct((split, split), jnp.float32)
    first_gram = Sum(first_gram)
    first_gram.over_row({2: b.arrived[:1]} if paired else {})
    if paired:
        second, mixed_gram = b.finish(first_gram.mine, first)
    first_gram.over_col()
    mixed_gram = Sum(mixed_gram)
    upper, inverse, first_basis = pl.pallas_call(
        functools.partial(first_factor_kernel, total_rows),
        out_shape=(square, square, jax.ShapeDtypeStruct(first.shape, jnp.float32)),
        compiler_params=params,
    )(first_gram.finish(), first)
    mixed_gram.over_row({4: upper})
    mixed_gram.over_col()
    return pl.pallas_call(
        functools.partial(second_factor_kernel, total_rows),
        out_shape=(
            jax.ShapeDtypeStruct((width, sketch_width), jnp.float32),
            jax.ShapeDtypeStruct((sketch_width, sketch_width), jnp.float32),
        ),
        compiler_params=params,
    )(mixed_gram.finish(), upper, inverse, first_basis, second)


def solution(mesh):
    return jax.shard_map(
        body,
        mesh=mesh,
        in_specs=(
            P("row", "col", None, None, None),
            P("row", "col", None),
            P("row", "col", None),
            P("row", "col"),
            P(("row", "col"), None),
        ),
        out_specs=(P(("row", "col"), None), P()),
        check_vma=False,
    )
```

```python
import functools
import jax
import jax.numpy as jnp
from jax import lax
from jax.experimental import pallas as pl
from jax.experimental.pallas import tpu as pltpu
from jax.sharding import PartitionSpec as P

BR = 12
BC = 12
GROUP = 16
SUBLANES = 8
VMEM_LIMIT = 52 * 1024 * 1024
NO_COST = pl.CostEstimate(flops=0, bytes_accessed=0, transcendentals=0)


def swap(value, axis, offset):
    size = lax.axis_size(axis)
    return lax.ppermute(value, axis, [(i, i ^ offset) for i in range(size)])


def fetch_tiles(count, tiles_ref, tile_buf, sems):
    slots = tiles_ref.shape[0]
    for slot in range(slots):
        @pl.when(slot < count)
        def _():
            pltpu.make_async_copy(tiles_ref.at[slot], tile_buf.at[slot], sems.at[slot]).start()


def for_each_tile(layout_ref, tiles_ref, tile_buf, sems, multiply, add, forward=False):
    slots = tiles_ref.shape[0]
    count = layout_ref[0]

    def wait(slot):
        pltpu.make_async_copy(tiles_ref.at[slot], tile_buf.at[slot], sems.at[slot]).wait()

    def step(pair, carry):
        slot = 2 * pair
        other = jnp.minimum(slot + 1, slots - 1)
        paired = slot + 1 < count
        wait(slot)

        @pl.when(paired)
        def _():
            wait(other)

        ends = [(layout_ref[1 + s], layout_ref[1 + slots + s]) for s in (slot, other)]
        (source, target), (other_source, other_target) = [end[::-1] if forward else end for end in ends]
        value = multiply(slot, source)
        other_value = multiply(other, other_source)
        add(target, value)
        add(other_target, jnp.where(paired, other_value, 0.0))
        return carry

    lax.fori_loop(0, (count + 1) // 2, step, 0)


def prepare_kernel(sketch_ref, *refs):
    urgent_ref, *half_refs, flipped = refs
    row_index = lax.axis_index("row")
    core, place = row_index % 2, row_index // 2
    places = lax.axis_size("row") // 2
    flipped[...] = sketch_ref[...].T

    def copy(target, index, half, which_core, offset):
        group = (half * 2 + (core ^ which_core)) * places + (place ^ offset)
        target[GROUP * index : GROUP * (index + 1), :] = flipped[
            pl.ds(pl.multiple_of(group * GROUP, GROUP), GROUP), :
        ]

    for which_core in range(2):
        for half, half_ref in enumerate(half_refs):
            copy(urgent_ref, which_core * len(half_refs) + half, half, which_core, places - 1)
            for offset in range(places - 1):
                copy(half_ref, which_core * (places - 1) + offset, half, which_core, offset)


def transposed_kernel(places, layout_ref, tiles_ref, *refs):
    *out_refs, sketch_buf, tile_buf, sems = refs[len(places) :]
    count = layout_ref[0]
    fetch_tiles(count, tiles_ref, tile_buf, sems)
    col_index = lax.axis_index("col")
    tile_size = tiles_ref.shape[1]
    for (offset, start), piece in zip(places, refs):
        depth, width = piece.shape
        lanes = pl.ds(pl.multiple_of((col_index ^ offset) * width, 128), width)
        if width == sketch_buf.shape[1]:
            lanes = slice(None)
        sketch_buf[start : start + depth, lanes] = piece[...]
    for out_ref in out_refs:
        out_ref[...] = jnp.zeros_like(out_ref)

    def multiply(slot, row):
        block = sketch_buf[:, pl.ds(pl.multiple_of(row * tile_size, 128), tile_size)]
        return jnp.dot(block, tile_buf[slot], preferred_element_type=jnp.float32)

    def add(col, value):
        lanes = pl.ds(pl.multiple_of(col * tile_size, 128), tile_size)
        depth = out_refs[0].shape[0]
        for i, out_ref in enumerate(out_refs):
            out_ref[:, lanes] += value[depth * i : depth * (i + 1)]

    for_each_tile(layout_ref, tiles_ref, tile_buf, sems, multiply, add)


def forward_kernel(outs, layout_ref, tiles_ref, *refs):
    column_buf, total, tile_buf, sems = refs[-4:]
    pieces, out_refs = refs[: -4 - outs], refs[-4 - outs : -4]
    count = layout_ref[0]
    fetch_tiles(count, tiles_ref, tile_buf, sems)
    row_index, col_index = lax.axis_index("row"), lax.axis_index("col")
    tile_size = tiles_ref.shape[1]
    half = len(pieces) // 2
    core, place = row_index % 2, row_index // 2
    for offset, piece in enumerate(pieces):
        if half:
            target = (core ^ (offset // half)) * half + (place ^ (offset % half))
            column_buf[pl.ds(pl.multiple_of(target * GROUP, GROUP), GROUP), :] = piece[...]
        else:
            column_buf[...] = piece[...]
    total[...] = jnp.zeros_like(total)

    def multiply(slot, col):
        block = column_buf[:, pl.ds(pl.multiple_of(col * tile_size, 128), tile_size)]
        return lax.dot_general(
            tile_buf[slot], block, (((1,), (1,)), ((), ())), preferred_element_type=jnp.float32
        )

    def add(row, value):
        total[pl.ds(pl.multiple_of(row * tile_size, 128), tile_size), :] += value

    for_each_tile(layout_ref, tiles_ref, tile_buf, sems, multiply, add, forward=True)
    for offset, out_ref in enumerate(out_refs):
        width = out_ref.shape[0]
        if outs == 1:
            out_ref[...] = total[...]
        else:
            start = pl.multiple_of((col_index ^ offset) * width, 128)
            out_ref[...] = total[pl.ds(start, width), :].astype(out_ref.dtype)


def tile_call(kernel, out_shape, scratch, layout, tiles, pieces):
    slots, tile_size, _ = tiles.shape
    smem = pl.BlockSpec(memory_space=pltpu.SMEM)
    vmem = pl.BlockSpec(memory_space=pltpu.VMEM)
    return pl.pallas_call(
        kernel,
        out_shape=out_shape,
        in_specs=[smem, pl.BlockSpec(memory_space=pl.ANY)] + [vmem] * len(pieces),
        out_specs=jax.tree.map(lambda _: vmem, out_shape),
        scratch_shapes=scratch
        + [
            pltpu.VMEM((slots, tile_size, tile_size), jnp.bfloat16),
            pltpu.SemaphoreType.DMA((slots,)),
        ],
        compiler_params=pltpu.CompilerParams(vmem_limit_bytes=VMEM_LIMIT),
        cost_estimate=NO_COST,
    )(layout, tiles, *pieces)


def after(value, token):
    return value if token is None else lax.optimization_barrier((value, token))[0]


def half(value):
    return value.astype(jnp.float16)


def full(value):
    return value.astype(jnp.float32)


def gather(shard):
    return [(0, 0, shard)] + [(d, 0, swap(shard, "col", d)) for d in range(1, lax.axis_size("col"))]


class Half:
    def __init__(self, call_transposed, call_forward, shard):
        self.call_transposed, self.call_forward = call_transposed, call_forward
        self.shard = shard

    def gather_near(self):
        self.middle = self.shard.shape[0] // 2
        parts = [self.shard[: self.middle], self.shard[self.middle :]]
        self.near = [[swap(part, "col", d) for part in parts] for d in (1, 2)]

    def gather_far(self):
        first, second = self.near
        self.pieces = [(0, 0, self.shard)]
        self.pieces += [(d, self.middle * i, part) for d in (1, 2) for i, part in enumerate(self.near[d - 1])]
        self.pieces.append((3, 0, swap(second[0], "col", 1)))
        self.pieces.append((3, self.middle, swap(first[1], "col", 2)))

    def multiply_transposed(self, token=None):
        self.mine, self.other = self.call_transposed(self.pieces, token)

    def send_other(self, token=None):
        self.arrived = swap(after(self.other, token), "row", 1)

    def reduce(self, far):
        rows = lambda value, d: value[d * GROUP : (d + 1) * GROUP]
        self.parts = [rows(self.mine, d) + rows(self.arrived, d) for d in range(3)]
        self.sent = half(self.parts[2] + full(far))
        middle = swap(self.sent, "row", 4)
        self.arriving = [middle]

    def reduce_last(self, token):
        self.arriving.append(swap(half(after(self.parts[1], token)), "row", 2))

    def own(self, token=None):
        middle, low = after(self.arriving, token)
        self.whole = {0: (self.parts[0] + full(middle) + full(low)).astype(jnp.bfloat16)}
        self.whole[2] = swap(self.whole[0], "row", 4)
        self.whole[1] = swap(self.whole[0], "row", 2)

    def spread(self, token=None):
        self.whole[2] = after(self.whole[2], token)
        self.whole[3] = swap(self.whole[2], "row", 2)

    def share(self, token=None):
        self.whole[1], self.whole[3] = after([self.whole[1], self.whole[3]], token)
        near = [self.whole[d] for d in range(4)]
        self.columns = near + [swap(v, "row", 1) for v in near]

    def multiply_forward(self, token=None):
        self.forward = self.call_forward(after(self.columns, token))

    def send_rows(self, token=None):
        self.total, *self.sent = after(self.forward, token)
        self.arrived = [swap(value, "col", d + 1) for d, value in enumerate(self.sent)]

    def finish(self, token=None, *others):
        return finish_call([self.total] + after(self.arrived, token), *others)


def finish_call(parts, *others):
    shape = parts[0].shape
    return pl.pallas_call(
        functools.partial(finish_kernel, len(parts)),
        out_shape=(
            jax.ShapeDtypeStruct(shape, jnp.float32),
            jax.ShapeDtypeStruct((shape[1] * (len(others) + 1), shape[1]), jnp.float32),
        ),
        compiler_params=pltpu.CompilerParams(vmem_limit_bytes=VMEM_LIMIT),
        cost_estimate=NO_COST,
    )(*others, *parts)


def run_pair(call_transposed, a, b, urgent):
    pieces = gather(urgent)
    a.gather_near()
    mine, other = call_transposed(pieces, None)
    arrived = swap(after(other, a.near), "row", 1)
    a.gather_far()
    b.shard = after(b.shard, a.near)
    b.gather_near()
    sent = half(mine + arrived)
    far = swap(sent, "row", 2)
    a.multiply_transposed(sent)
    a.send_other([b.near, far])
    b.gather_far()
    a.reduce(far[:GROUP])
    a.reduce_last(a.sent)
    b.multiply_transposed(a.sent)
    b.send_other(a.arriving[0])
    a.own(b.other)
    b.reduce(after(far[GROUP:], a.whole[0]))
    a.spread(b.sent)
    b.reduce_last(a.whole[3])
    a.share()
    a.multiply_forward()
    b.own(a.forward)
    a.send_rows()
    b.spread(a.arrived[:2])
    b.share()
    b.multiply_forward()
    b.send_rows(a.arrived[2:])


class Sum:
    def __init__(self, value):
        half = value.shape[0] // 2
        self.core = lax.axis_index("row") % 2
        mine = lax.dynamic_slice_in_dim(value, self.core * half, half, 0)
        other = lax.dynamic_slice_in_dim(value, (1 - self.core) * half, half, 0)
        self.mine = mine + swap(other, "row", 1)

    def over_row(self, tokens):
        bit = 2
        while bit < lax.axis_size("row"):
            self.mine = self.mine + after(swap(self.mine, "row", bit), tokens.get(bit))
            bit *= 2

    def over_col(self, token=None):
        mine = after(self.mine, token)
        arrived = [swap(mine, "col", d) for d in range(1, lax.axis_size("col"))]
        stack = jnp.stack([mine] + arrived)
        self.mine = sum(
            lax.dynamic_index_in_dim(stack, lax.axis_index("col") ^ d, 0, keepdims=False)
            for d in range(lax.axis_size("col"))
        )

    def finish(self):
        other = swap(self.mine, "row", 1)
        return jnp.where(
            self.core == 0, jnp.concatenate([self.mine, other]), jnp.concatenate([other, self.mine])
        )


def product(left, right, left_dim, right_dim):
    return lax.dot_general(
        left, right, (((left_dim,), (right_dim,)), ((), ())),
        precision=lax.Precision.HIGHEST, preferred_element_type=jnp.float32,
    )


def finish_kernel(parts, *refs):
    rows_ref, gram_ref = refs[-2:]
    others, parts = refs[: -2 - parts], refs[-2 - parts : -2]
    total = parts[0][...]
    for part in parts[1:]:
        total = total + part[...].astype(jnp.float32)
    rows_ref[...] = total
    size = total.shape[1]
    for i, other in enumerate(others):
        gram_ref[size * i : size * (i + 1), :] = product(other[...], total, 0, 0)
    gram_ref[size * len(others) :, :] = product(total, total, 0, 0)


def factor_with_inverse(matrix):
    size = matrix.shape[1]
    groups = size // SUBLANES
    shape = (SUBLANES, size)
    row = lax.broadcasted_iota(jnp.int32, shape, 0)
    col = lax.broadcasted_iota(jnp.int32, shape, 1)
    left = [matrix[SUBLANES * g : SUBLANES * (g + 1), :] for g in range(groups)]
    right = [(col == row + SUBLANES * g).astype(jnp.float32) for g in range(groups)]
    spread = lambda value, j: jnp.broadcast_to(value[j : j + 1, :], shape)
    for p in range(groups):
        columns = [
            {
                g: jnp.broadcast_to(left[g][:, SUBLANES * p + k : SUBLANES * p + k + 1], shape)
                for g in range(p, groups)
            }
            for k in range(SUBLANES)
        ]
        pivots = None
        for j in range(SUBLANES):
            pivot = spread(columns[j][p], j)
            inverse = 1.0 / pivot
            pivots = pivot if pivots is None else jnp.where(row == j, pivot, pivots)
            left_row, right_row = spread(left[p], j), spread(right[p], j)
            heads = {k: spread(columns[k][p], j) for k in range(j + 1, SUBLANES)}
            for g in range(p, groups):
                scale = columns[j][g] * inverse
                if g == p:
                    scale = jnp.where(row > j, scale, 0.0)
                left[g] = left[g] - scale * left_row
                right[g] = right[g] - scale * right_row
                for k, head in heads.items():
                    columns[k][g] = columns[k][g] - scale * head
        scale = lax.rsqrt(pivots)
        left[p] = jnp.where(col >= row + SUBLANES * p, left[p] * scale, 0.0)
        right[p] = right[p] * scale
    return jnp.concatenate(left), jnp.concatenate(right)


def first_factor_kernel(total_rows, gram_ref, rows_ref, upper_ref, inverse_ref, basis_ref):
    upper, inverse = factor_with_inverse(gram_ref[...] / total_rows)
    upper_ref[...] = upper
    inverse_ref[...] = inverse
    basis_ref[...] = product(rows_ref[...], inverse, 1, 1)


def second_factor_kernel(
    total_rows, gram_ref, upper_ref, inverse_ref, first_ref, rows_ref, basis_ref, factor_ref
):
    split = upper_ref.shape[0]
    mixed, last = gram_ref[:split] / total_rows, gram_ref[split:] / total_rows
    corner = product(inverse_ref[...], mixed, 1, 0)
    upper, inverse = factor_with_inverse(last - product(corner, corner, 0, 0))
    factor_ref[:split, :split] = upper_ref[...]
    factor_ref[:split, split:] = corner
    factor_ref[split:, :split] = jnp.zeros_like(upper)
    factor_ref[split:, split:] = upper
    first = first_ref[...]
    basis_ref[:, :split] = first
    basis_ref[:, split:] = product(rows_ref[...], inverse, 1, 1) - product(
        first, product(corner, inverse, 1, 1), 1, 0
    )


def body(tiles, tile_rows, tile_cols, tile_counts, sketch):
    tiles = tiles[0, 0]
    layout = jnp.concatenate([tile_counts[0], tile_rows[0, 0], tile_cols[0, 0]])
    slots, tile_size, _ = tiles.shape
    width, sketch_width = sketch.shape
    group_rows, group_cols = BR * tile_size, BC * tile_size
    split = sketch_width // 2
    rows_axis, cols_axis = lax.axis_size("row"), lax.axis_size("col")

    def call_transposed(pieces, token):
        depth = pieces[0][2].shape[0]
        outs = 2 if rows_axis == 8 else 1
        return tile_call(
            functools.partial(transposed_kernel, [piece[:2] for piece in pieces]),
            [jax.ShapeDtypeStruct((depth // outs, group_cols), jnp.float32)] * outs,
            [pltpu.VMEM((depth, group_rows), jnp.bfloat16)],
            layout, tiles, after([piece[2] for piece in pieces], token),
        )

    def call_forward(columns, outs=cols_axis):
        depth = sum(piece.shape[0] for piece in columns)
        return tile_call(
            functools.partial(forward_kernel, outs),
            [
                jax.ShapeDtypeStruct((group_rows // outs, depth), jnp.bfloat16 if offset else jnp.float32)
                for offset in range(outs)
            ],
            [pltpu.VMEM((depth, group_cols), jnp.bfloat16), pltpu.VMEM((group_rows, depth), jnp.float32)],
            layout, tiles, columns,
        )

    paired = rows_axis == 8 and cols_axis == 4 and sketch_width == 2 * GROUP * rows_axis
    if paired:
        part = lambda groups: jax.ShapeDtypeStruct((groups * GROUP, width), jnp.bfloat16)
        urgent, *halves = pl.pallas_call(
            prepare_kernel,
            out_shape=[part(4), part(6), part(6)],
            scratch_shapes=[pltpu.VMEM((sketch_width, width), jnp.bfloat16)],
            compiler_params=pltpu.CompilerParams(vmem_limit_bytes=VMEM_LIMIT),
            cost_estimate=NO_COST,
        )(sketch)
        a, b = [Half(call_transposed, call_forward, shard) for shard in halves]
        run_pair(call_transposed, a, b, urgent)
        first, first_gram = a.finish(b.sent)
    else:
        everything = lax.all_gather(sketch.T, "col", axis=1, tiled=True)
        (partial,) = call_transposed([(0, 0, everything)], None)
        columns = lax.psum_scatter(partial, "row", scatter_dimension=0, tiled=True).astype(jnp.bfloat16)
        columns = lax.all_gather(columns, "row", axis=0, tiled=True)
        (partial,) = call_forward([columns], 1)
        whole, gram = finish_call([lax.psum_scatter(partial, "col", scatter_dimension=0, tiled=True)])
        first, second = whole[:, :split], whole[:, split:]
        first_gram, mixed_gram = gram[:split, :split], gram[:, split:]
    total_rows = group_rows * lax.axis_size("row")
    params = pltpu.CompilerParams(vmem_limit_bytes=VMEM_LIMIT)
    square = jax.ShapeDtypeStruct((split, split), jnp.float32)
    first_gram = Sum(first_gram)
    first_gram.over_row({2: b.arrived[:1]} if paired else {})
    if paired:
        second, mixed_gram = b.finish(first_gram.mine, first)
    first_gram.over_col()
    mixed_gram = Sum(mixed_gram)
    upper, inverse, first_basis = pl.pallas_call(
        functools.partial(first_factor_kernel, total_rows),
        out_shape=(square, square, jax.ShapeDtypeStruct(first.shape, jnp.float32)),
        compiler_params=params,
    )(first_gram.finish(), first)
    mixed_gram.over_row({4: upper})
    mixed_gram.over_col()
    return pl.pallas_call(
        functools.partial(second_factor_kernel, total_rows),
        out_shape=(
            jax.ShapeDtypeStruct((width, sketch_width), jnp.float32),
            jax.ShapeDtypeStruct((sketch_width, sketch_width), jnp.float32),
        ),
        compiler_params=params,
    )(mixed_gram.finish(), upper, inverse, first_basis, second)


def solution(mesh):
    return jax.shard_map(
        body,
        mesh=mesh,
        in_specs=(
            P("row", "col", None, None, None),
            P("row", "col", None),
            P("row", "col", None),
            P("row", "col"),
            P(("row", "col"), None),
        ),
        out_specs=(P(("row", "col"), None), P()),
        check_vma=False,
    )
```

```python
import functools
import jax
import jax.numpy as jnp
from jax import lax
from jax.experimental import pallas as pl
from jax.experimental.pallas import tpu as pltpu
from jax.sharding import PartitionSpec as P

BR = 12
BC = 12
GROUP = 16
SUBLANES = 8
SCALE = 16.0
VMEM_LIMIT = 52 * 1024 * 1024
NO_COST = pl.CostEstimate(flops=0, bytes_accessed=0, transcendentals=0)


def swap(value, axis, offset):
    size = lax.axis_size(axis)
    return lax.ppermute(value, axis, [(i, i ^ offset) for i in range(size)])


def fetch_tiles(count, tiles_ref, tile_buf, sems):
    slots = tiles_ref.shape[0]
    for slot in range(slots):
        @pl.when(slot < count)
        def _():
            pltpu.make_async_copy(tiles_ref.at[slot], tile_buf.at[slot], sems.at[slot]).start()


def for_each_tile(layout_ref, tiles_ref, tile_buf, sems, multiply, add, forward=False):
    slots = tiles_ref.shape[0]
    count = layout_ref[0]

    def wait(slot):
        pltpu.make_async_copy(tiles_ref.at[slot], tile_buf.at[slot], sems.at[slot]).wait()

    def step(pair, carry):
        slot = 2 * pair
        other = jnp.minimum(slot + 1, slots - 1)
        paired = slot + 1 < count
        wait(slot)

        @pl.when(paired)
        def _():
            wait(other)

        ends = [(layout_ref[1 + s], layout_ref[1 + slots + s]) for s in (slot, other)]
        (source, target), (other_source, other_target) = [end[::-1] if forward else end for end in ends]
        value = multiply(slot, source)
        other_value = multiply(other, other_source)
        add(target, value)
        add(other_target, jnp.where(paired, other_value, 0.0))
        return carry

    lax.fori_loop(0, (count + 1) // 2, step, 0)


def prepare_kernel(sketch_ref, *refs):
    urgent_ref, *half_refs, flipped = refs
    row_index = lax.axis_index("row")
    core, place = row_index % 2, row_index // 2
    places = lax.axis_size("row") // 2
    flipped[...] = sketch_ref[...].T

    def copy(target, index, half, which_core, offset):
        group = (half * 2 + (core ^ which_core)) * places + (place ^ offset)
        target[GROUP * index : GROUP * (index + 1), :] = flipped[
            pl.ds(pl.multiple_of(group * GROUP, GROUP), GROUP), :
        ]

    for which_core in range(2):
        for half, half_ref in enumerate(half_refs):
            copy(urgent_ref, which_core * len(half_refs) + half, half, which_core, places - 1)
            for offset in range(places - 1):
                copy(half_ref, which_core * (places - 1) + offset, half, which_core, offset)


def transposed_kernel(places, layout_ref, tiles_ref, *refs):
    *out_refs, sketch_buf, tile_buf, sems = refs[len(places) :]
    count = layout_ref[0]
    fetch_tiles(count, tiles_ref, tile_buf, sems)
    col_index = lax.axis_index("col")
    tile_size = tiles_ref.shape[1]
    for (offset, start), piece in zip(places, refs):
        depth, width = piece.shape
        lanes = pl.ds(pl.multiple_of((col_index ^ offset) * width, 128), width)
        if width == sketch_buf.shape[1]:
            lanes = slice(None)
        sketch_buf[start : start + depth, lanes] = piece[...]
    for out_ref in out_refs:
        out_ref[...] = jnp.zeros_like(out_ref)

    def multiply(slot, row):
        block = sketch_buf[:, pl.ds(pl.multiple_of(row * tile_size, 128), tile_size)]
        return jnp.dot(block, tile_buf[slot], preferred_element_type=jnp.float32)

    def add(col, value):
        lanes = pl.ds(pl.multiple_of(col * tile_size, 128), tile_size)
        depth = out_refs[0].shape[0]
        for i, out_ref in enumerate(out_refs):
            out_ref[:, lanes] += value[depth * i : depth * (i + 1)]

    for_each_tile(layout_ref, tiles_ref, tile_buf, sems, multiply, add)


def forward_kernel(outs, layout_ref, tiles_ref, *refs):
    column_buf, total, tile_buf, sems = refs[-4:]
    pieces, out_refs = refs[: -4 - outs], refs[-4 - outs : -4]
    count = layout_ref[0]
    fetch_tiles(count, tiles_ref, tile_buf, sems)
    row_index, col_index = lax.axis_index("row"), lax.axis_index("col")
    tile_size = tiles_ref.shape[1]
    half = len(pieces) // 2
    core, place = row_index % 2, row_index // 2
    for offset, piece in enumerate(pieces):
        if half:
            target = (core ^ (offset // half)) * half + (place ^ (offset % half))
            column_buf[pl.ds(pl.multiple_of(target * GROUP, GROUP), GROUP), :] = piece[...]
        else:
            column_buf[...] = piece[...]
    total[...] = jnp.zeros_like(total)

    def multiply(slot, col):
        block = column_buf[:, pl.ds(pl.multiple_of(col * tile_size, 128), tile_size)]
        return lax.dot_general(
            tile_buf[slot], block, (((1,), (1,)), ((), ())), preferred_element_type=jnp.float32
        )

    def add(row, value):
        total[pl.ds(pl.multiple_of(row * tile_size, 128), tile_size), :] += value

    for_each_tile(layout_ref, tiles_ref, tile_buf, sems, multiply, add, forward=True)
    for offset, out_ref in enumerate(out_refs):
        width = out_ref.shape[0]
        if outs == 1:
            out_ref[...] = total[...]
        else:
            start = pl.multiple_of((col_index ^ offset) * width, 128)
            out_ref[...] = total[pl.ds(start, width), :].astype(out_ref.dtype)


def tile_call(kernel, out_shape, scratch, layout, tiles, pieces):
    slots, tile_size, _ = tiles.shape
    smem = pl.BlockSpec(memory_space=pltpu.SMEM)
    vmem = pl.BlockSpec(memory_space=pltpu.VMEM)
    return pl.pallas_call(
        kernel,
        out_shape=out_shape,
        in_specs=[smem, pl.BlockSpec(memory_space=pl.ANY)] + [vmem] * len(pieces),
        out_specs=jax.tree.map(lambda _: vmem, out_shape),
        scratch_shapes=scratch
        + [
            pltpu.VMEM((slots, tile_size, tile_size), jnp.bfloat16),
            pltpu.SemaphoreType.DMA((slots,)),
        ],
        compiler_params=pltpu.CompilerParams(vmem_limit_bytes=VMEM_LIMIT),
        cost_estimate=NO_COST,
    )(layout, tiles, *pieces)


def after(value, token):
    return value if token is None else lax.optimization_barrier((value, token))[0]


def half(value):
    return (value * (1.0 / SCALE)).astype(jnp.float16)


def full(value):
    return value.astype(jnp.float32) * SCALE


def gather(shard):
    return [(0, 0, shard)] + [(d, 0, swap(shard, "col", d)) for d in range(1, lax.axis_size("col"))]


class Half:
    def __init__(self, call_transposed, call_forward, shard):
        self.call_transposed, self.call_forward = call_transposed, call_forward
        self.shard = shard

    def gather_near(self):
        self.middle = self.shard.shape[0] // 2
        parts = [self.shard[: self.middle], self.shard[self.middle :]]
        self.near = [[swap(part, "col", d) for part in parts] for d in (1, 2)]

    def gather_far(self):
        first, second = self.near
        self.pieces = [(0, 0, self.shard)]
        self.pieces += [(d, self.middle * i, part) for d in (1, 2) for i, part in enumerate(self.near[d - 1])]
        self.pieces.append((3, 0, swap(second[0], "col", 1)))
        self.pieces.append((3, self.middle, swap(first[1], "col", 2)))

    def multiply_transposed(self, token=None):
        self.mine, self.other = self.call_transposed(self.pieces, token)

    def send_other(self, token=None):
        self.arrived = swap(after(self.other, token), "row", 1)

    def reduce(self, far):
        rows = lambda value, d: value[d * GROUP : (d + 1) * GROUP]
        self.parts = [rows(self.mine, d) + rows(self.arrived, d) for d in range(3)]
        self.sent = half(self.parts[2] + full(far))
        middle = swap(self.sent, "row", 4)
        self.arriving = [middle]

    def reduce_last(self, token):
        self.arriving.append(swap(half(after(self.parts[1], token)), "row", 2))

    def own(self, token=None):
        middle, low = after(self.arriving, token)
        self.whole = {0: (self.parts[0] + full(middle) + full(low)).astype(jnp.bfloat16)}
        self.whole[2] = swap(self.whole[0], "row", 4)
        self.whole[1] = swap(self.whole[0], "row", 2)

    def spread(self, token=None):
        self.whole[2] = after(self.whole[2], token)
        self.whole[3] = swap(self.whole[2], "row", 2)

    def share(self, token=None):
        self.whole[1], self.whole[3] = after([self.whole[1], self.whole[3]], token)
        near = [self.whole[d] for d in range(4)]
        self.columns = near + [swap(v, "row", 1) for v in near]

    def multiply_forward(self, token=None):
        self.forward = self.call_forward(after(self.columns, token))

    def send_rows(self, token=None):
        self.total, *self.sent = after(self.forward, token)
        self.arrived = [swap(value, "col", d + 1) for d, value in enumerate(self.sent)]

    def finish(self, token=None, *others):
        return finish_call([self.total] + after(self.arrived, token), *others)


def finish_call(parts, *others):
    shape = parts[0].shape
    return pl.pallas_call(
        functools.partial(finish_kernel, len(parts)),
        out_shape=(
            jax.ShapeDtypeStruct(shape, jnp.float32),
            jax.ShapeDtypeStruct((shape[1] * (len(others) + 1), shape[1]), jnp.float32),
        ),
        compiler_params=pltpu.CompilerParams(vmem_limit_bytes=VMEM_LIMIT),
        cost_estimate=NO_COST,
    )(*others, *parts)


def run_pair(call_transposed, a, b, urgent):
    pieces = gather(urgent)
    a.gather_near()
    mine, other = call_transposed(pieces, None)
    arrived = swap(after(other, a.near), "row", 1)
    a.gather_far()
    b.shard = after(b.shard, a.near)
    b.gather_near()
    sent = half(mine + arrived)
    far = swap(sent, "row", 2)
    a.multiply_transposed(sent)
    a.send_other([b.near, far])
    b.gather_far()
    a.reduce(far[:GROUP])
    a.reduce_last([a.sent, [piece[2] for piece in b.pieces[5:]]])
    b.multiply_transposed(a.sent)
    b.send_other(a.arriving[0])
    a.own(b.other)
    b.reduce(after(far[GROUP:], a.whole[0]))
    a.spread(b.sent)
    b.reduce_last(a.whole[3])
    a.share()
    a.multiply_forward()
    b.own(a.forward)
    a.send_rows()
    b.spread()
    b.share(a.arrived[:2])
    b.multiply_forward()
    b.send_rows(a.arrived[2:])


class Sum:
    def __init__(self, value):
        half = value.shape[0] // 2
        self.core = lax.axis_index("row") % 2
        mine = lax.dynamic_slice_in_dim(value, self.core * half, half, 0)
        other = lax.dynamic_slice_in_dim(value, (1 - self.core) * half, half, 0)
        self.mine = mine + swap(other, "row", 1)

    def over_row(self, tokens):
        bit = 2
        while bit < lax.axis_size("row"):
            self.mine = self.mine + after(swap(self.mine, "row", bit), tokens.get(bit))
            bit *= 2

    def over_col(self, token=None):
        mine = after(self.mine, token)
        arrived = [swap(mine, "col", d) for d in range(1, lax.axis_size("col"))]
        stack = jnp.stack([mine] + arrived)
        self.mine = sum(
            lax.dynamic_index_in_dim(stack, lax.axis_index("col") ^ d, 0, keepdims=False)
            for d in range(lax.axis_size("col"))
        )

    def finish(self):
        other = swap(self.mine, "row", 1)
        return jnp.where(
            self.core == 0, jnp.concatenate([self.mine, other]), jnp.concatenate([other, self.mine])
        )


def product(left, right, left_dim, right_dim):
    return lax.dot_general(
        left, right, (((left_dim,), (right_dim,)), ((), ())),
        precision=lax.Precision.HIGHEST, preferred_element_type=jnp.float32,
    )


def finish_kernel(parts, *refs):
    rows_ref, gram_ref = refs[-2:]
    others, parts = refs[: -2 - parts], refs[-2 - parts : -2]
    total = parts[0][...]
    for part in parts[1:]:
        total = total + part[...].astype(jnp.float32)
    rows_ref[...] = total
    size = total.shape[1]
    for i, other in enumerate(others):
        gram_ref[size * i : size * (i + 1), :] = product(other[...], total, 0, 0)
    gram_ref[size * len(others) :, :] = product(total, total, 0, 0)


def factor_with_inverse(matrix):
    size = matrix.shape[1]
    groups = size // SUBLANES
    shape = (SUBLANES, size)
    row = lax.broadcasted_iota(jnp.int32, shape, 0)
    col = lax.broadcasted_iota(jnp.int32, shape, 1)
    left = [matrix[SUBLANES * g : SUBLANES * (g + 1), :] for g in range(groups)]
    right = [(col == row + SUBLANES * g).astype(jnp.float32) for g in range(groups)]
    spread = lambda value, j: jnp.broadcast_to(value[j : j + 1, :], shape)
    for p in range(groups):
        columns = [
            {
                g: jnp.broadcast_to(left[g][:, SUBLANES * p + k : SUBLANES * p + k + 1], shape)
                for g in range(p, groups)
            }
            for k in range(SUBLANES)
        ]
        pivots = None
        for j in range(SUBLANES):
            pivot = spread(columns[j][p], j)
            inverse = 1.0 / pivot
            pivots = pivot if pivots is None else jnp.where(row == j, pivot, pivots)
            left_row, right_row = spread(left[p], j), spread(right[p], j)
            heads = {k: spread(columns[k][p], j) for k in range(j + 1, SUBLANES)}
            for g in range(p, groups):
                scale = columns[j][g] * inverse
                if g == p:
                    scale = jnp.where(row > j, scale, 0.0)
                left[g] = left[g] - scale * left_row
                right[g] = right[g] - scale * right_row
                for k, head in heads.items():
                    columns[k][g] = columns[k][g] - scale * head
        scale = lax.rsqrt(pivots)
        left[p] = jnp.where(col >= row + SUBLANES * p, left[p] * scale, 0.0)
        right[p] = right[p] * scale
    return jnp.concatenate(left), jnp.concatenate(right)


def first_factor_kernel(total_rows, gram_ref, rows_ref, upper_ref, inverse_ref, basis_ref):
    upper, inverse = factor_with_inverse(gram_ref[...] / total_rows)
    upper_ref[...] = upper
    inverse_ref[...] = inverse
    basis_ref[...] = product(rows_ref[...], inverse, 1, 1)


def second_factor_kernel(
    total_rows, gram_ref, upper_ref, inverse_ref, first_ref, rows_ref, basis_ref, factor_ref
):
    split = upper_ref.shape[0]
    mixed, last = gram_ref[:split] / total_rows, gram_ref[split:] / total_rows
    corner = product(inverse_ref[...], mixed, 1, 0)
    upper, inverse = factor_with_inverse(last - product(corner, corner, 0, 0))
    factor_ref[:split, :split] = upper_ref[...]
    factor_ref[:split, split:] = corner
    factor_ref[split:, :split] = jnp.zeros_like(upper)
    factor_ref[split:, split:] = upper
    first = first_ref[...]
    basis_ref[:, :split] = first
    basis_ref[:, split:] = product(rows_ref[...], inverse, 1, 1) - product(
        first, product(corner, inverse, 1, 1), 1, 0
    )


def body(tiles, tile_rows, tile_cols, tile_counts, sketch):
    tiles = tiles[0, 0]
    layout = jnp.concatenate([tile_counts[0], tile_rows[0, 0], tile_cols[0, 0]])
    slots, tile_size, _ = tiles.shape
    width, sketch_width = sketch.shape
    group_rows, group_cols = BR * tile_size, BC * tile_size
    split = sketch_width // 2
    rows_axis, cols_axis = lax.axis_size("row"), lax.axis_size("col")

    def call_transposed(pieces, token):
        depth = pieces[0][2].shape[0]
        outs = 2 if rows_axis == 8 else 1
        return tile_call(
            functools.partial(transposed_kernel, [piece[:2] for piece in pieces]),
            [jax.ShapeDtypeStruct((depth // outs, group_cols), jnp.float32)] * outs,
            [pltpu.VMEM((depth, group_rows), jnp.bfloat16)],
            layout, tiles, after([piece[2] for piece in pieces], token),
        )

    def call_forward(columns, outs=cols_axis):
        depth = sum(piece.shape[0] for piece in columns)
        return tile_call(
            functools.partial(forward_kernel, outs),
            [
                jax.ShapeDtypeStruct((group_rows // outs, depth), jnp.bfloat16 if offset else jnp.float32)
                for offset in range(outs)
            ],
            [pltpu.VMEM((depth, group_cols), jnp.bfloat16), pltpu.VMEM((group_rows, depth), jnp.float32)],
            layout, tiles, columns,
        )

    paired = rows_axis == 8 and cols_axis == 4 and sketch_width == 2 * GROUP * rows_axis
    if paired:
        part = lambda groups: jax.ShapeDtypeStruct((groups * GROUP, width), jnp.bfloat16)
        urgent, *halves = pl.pallas_call(
            prepare_kernel,
            out_shape=[part(4), part(6), part(6)],
            scratch_shapes=[pltpu.VMEM((sketch_width, width), jnp.bfloat16)],
            compiler_params=pltpu.CompilerParams(vmem_limit_bytes=VMEM_LIMIT),
            cost_estimate=NO_COST,
        )(sketch)
        a, b = [Half(call_transposed, call_forward, shard) for shard in halves]
        run_pair(call_transposed, a, b, urgent)
        first, first_gram = a.finish(b.sent)
    else:
        everything = lax.all_gather(sketch.T, "col", axis=1, tiled=True)
        (partial,) = call_transposed([(0, 0, everything)], None)
        columns = lax.psum_scatter(partial, "row", scatter_dimension=0, tiled=True).astype(jnp.bfloat16)
        columns = lax.all_gather(columns, "row", axis=0, tiled=True)
        (partial,) = call_forward([columns], 1)
        whole, gram = finish_call([lax.psum_scatter(partial, "col", scatter_dimension=0, tiled=True)])
        first, second = whole[:, :split], whole[:, split:]
        first_gram, mixed_gram = gram[:split, :split], gram[:, split:]
    total_rows = group_rows * lax.axis_size("row")
    params = pltpu.CompilerParams(vmem_limit_bytes=VMEM_LIMIT)
    square = jax.ShapeDtypeStruct((split, split), jnp.float32)
    first_gram = Sum(first_gram)
    first_gram.over_row({2: b.arrived[:1]} if paired else {})
    if paired:
        second, mixed_gram = b.finish(first_gram.mine, first)
    first_gram.over_col()
    mixed_gram = Sum(mixed_gram)
    upper, inverse, first_basis = pl.pallas_call(
        functools.partial(first_factor_kernel, total_rows),
        out_shape=(square, square, jax.ShapeDtypeStruct(first.shape, jnp.float32)),
        compiler_params=params,
    )(first_gram.finish(), first)
    mixed_gram.over_row({4: upper})
    mixed_gram.over_col()
    return pl.pallas_call(
        functools.partial(second_factor_kernel, total_rows),
        out_shape=(
            jax.ShapeDtypeStruct((width, sketch_width), jnp.float32),
            jax.ShapeDtypeStruct((sketch_width, sketch_width), jnp.float32),
        ),
        compiler_params=params,
    )(mixed_gram.finish(), upper, inverse, first_basis, second)


def solution(mesh):
    return jax.shard_map(
        body,
        mesh=mesh,
        in_specs=(
            P("row", "col", None, None, None),
            P("row", "col", None),
            P("row", "col", None),
            P("row", "col"),
            P(("row", "col"), None),
        ),
        out_specs=(P(("row", "col"), None), P()),
        check_vma=False,
    )
```

```python
import functools
import jax
import jax.numpy as jnp
from jax import lax
from jax.experimental import pallas as pl
from jax.experimental.pallas import tpu as pltpu
from jax.sharding import PartitionSpec as P

BR = 12
BC = 12
GROUP = 16
SUBLANES = 8
SCALE = 16.0
VMEM_LIMIT = 52 * 1024 * 1024
NO_COST = pl.CostEstimate(flops=0, bytes_accessed=0, transcendentals=0)


def swap(value, axis, offset):
    size = lax.axis_size(axis)
    return lax.ppermute(value, axis, [(i, i ^ offset) for i in range(size)])


def fetch_tiles(count, tiles_ref, tile_buf, sems):
    slots = tiles_ref.shape[0]
    for slot in range(slots):
        @pl.when(slot < count)
        def _():
            pltpu.make_async_copy(tiles_ref.at[slot], tile_buf.at[slot], sems.at[slot]).start()


def for_each_tile(layout_ref, tiles_ref, tile_buf, sems, multiply, add, forward=False):
    slots = tiles_ref.shape[0]
    count = layout_ref[0]

    def wait(slot):
        pltpu.make_async_copy(tiles_ref.at[slot], tile_buf.at[slot], sems.at[slot]).wait()

    def step(pair, carry):
        slot = 2 * pair
        other = jnp.minimum(slot + 1, slots - 1)
        paired = slot + 1 < count
        wait(slot)

        @pl.when(paired)
        def _():
            wait(other)

        ends = [(layout_ref[1 + s], layout_ref[1 + slots + s]) for s in (slot, other)]
        (source, target), (other_source, other_target) = [end[::-1] if forward else end for end in ends]
        value = multiply(slot, source)
        other_value = multiply(other, other_source)
        add(target, value)
        add(other_target, jnp.where(paired, other_value, 0.0))
        return carry

    lax.fori_loop(0, (count + 1) // 2, step, 0)


def prepare_kernel(sketch_ref, *refs):
    urgent_ref, *half_refs, flipped = refs
    row_index = lax.axis_index("row")
    core, place = row_index % 2, row_index // 2
    places = lax.axis_size("row") // 2
    flipped[...] = sketch_ref[...].T

    def copy(target, index, half, which_core, offset):
        group = (half * 2 + (core ^ which_core)) * places + (place ^ offset)
        target[GROUP * index : GROUP * (index + 1), :] = flipped[
            pl.ds(pl.multiple_of(group * GROUP, GROUP), GROUP), :
        ]

    for which_core in range(2):
        for half, half_ref in enumerate(half_refs):
            copy(urgent_ref, which_core * len(half_refs) + half, half, which_core, places - 1)
            for offset in range(places - 1):
                copy(half_ref, which_core * (places - 1) + offset, half, which_core, offset)


def transposed_kernel(places, layout_ref, tiles_ref, *refs):
    *out_refs, sketch_buf, tile_buf, sems = refs[len(places) :]
    count = layout_ref[0]
    fetch_tiles(count, tiles_ref, tile_buf, sems)
    col_index = lax.axis_index("col")
    tile_size = tiles_ref.shape[1]
    for (offset, start), piece in zip(places, refs):
        depth, width = piece.shape
        lanes = pl.ds(pl.multiple_of((col_index ^ offset) * width, 128), width)
        if width == sketch_buf.shape[1]:
            lanes = slice(None)
        sketch_buf[start : start + depth, lanes] = piece[...]
    for out_ref in out_refs:
        out_ref[...] = jnp.zeros_like(out_ref)

    def multiply(slot, row):
        block = sketch_buf[:, pl.ds(pl.multiple_of(row * tile_size, 128), tile_size)]
        return jnp.dot(block, tile_buf[slot], preferred_element_type=jnp.float32)

    def add(col, value):
        lanes = pl.ds(pl.multiple_of(col * tile_size, 128), tile_size)
        depth = out_refs[0].shape[0]
        for i, out_ref in enumerate(out_refs):
            out_ref[:, lanes] += value[depth * i : depth * (i + 1)]

    for_each_tile(layout_ref, tiles_ref, tile_buf, sems, multiply, add)


def forward_kernel(outs, layout_ref, tiles_ref, *refs):
    column_buf, total, tile_buf, sems = refs[-4:]
    pieces, out_refs = refs[: -4 - outs], refs[-4 - outs : -4]
    count = layout_ref[0]
    fetch_tiles(count, tiles_ref, tile_buf, sems)
    row_index, col_index = lax.axis_index("row"), lax.axis_index("col")
    tile_size = tiles_ref.shape[1]
    half = len(pieces) // 2
    core, place = row_index % 2, row_index // 2
    for offset, piece in enumerate(pieces):
        if half:
            target = (core ^ (offset // half)) * half + (place ^ (offset % half))
            column_buf[pl.ds(pl.multiple_of(target * GROUP, GROUP), GROUP), :] = piece[...]
        else:
            column_buf[...] = piece[...]
    total[...] = jnp.zeros_like(total)

    def multiply(slot, col):
        block = column_buf[:, pl.ds(pl.multiple_of(col * tile_size, 128), tile_size)]
        return lax.dot_general(
            tile_buf[slot], block, (((1,), (1,)), ((), ())), preferred_element_type=jnp.float32
        )

    def add(row, value):
        total[pl.ds(pl.multiple_of(row * tile_size, 128), tile_size), :] += value

    for_each_tile(layout_ref, tiles_ref, tile_buf, sems, multiply, add, forward=True)
    for offset, out_ref in enumerate(out_refs):
        width = out_ref.shape[0]
        if outs == 1:
            out_ref[...] = total[...]
        else:
            start = pl.multiple_of((col_index ^ offset) * width, 128)
            out_ref[...] = total[pl.ds(start, width), :].astype(out_ref.dtype)


def tile_call(kernel, out_shape, scratch, layout, tiles, pieces):
    slots, tile_size, _ = tiles.shape
    smem = pl.BlockSpec(memory_space=pltpu.SMEM)
    vmem = pl.BlockSpec(memory_space=pltpu.VMEM)
    return pl.pallas_call(
        kernel,
        out_shape=out_shape,
        in_specs=[smem, pl.BlockSpec(memory_space=pl.ANY)] + [vmem] * len(pieces),
        out_specs=jax.tree.map(lambda _: vmem, out_shape),
        scratch_shapes=scratch
        + [
            pltpu.VMEM((slots, tile_size, tile_size), jnp.bfloat16),
            pltpu.SemaphoreType.DMA((slots,)),
        ],
        compiler_params=pltpu.CompilerParams(vmem_limit_bytes=VMEM_LIMIT),
        cost_estimate=NO_COST,
    )(layout, tiles, *pieces)


def after(value, token):
    return value if token is None else lax.optimization_barrier((value, token))[0]


def half(value):
    return (value * (1.0 / SCALE)).astype(jnp.float16)


def full(value):
    return value.astype(jnp.float32) * SCALE


def gather(shard):
    return [(0, 0, shard)] + [(d, 0, swap(shard, "col", d)) for d in range(1, lax.axis_size("col"))]


class Half:
    def __init__(self, call_transposed, call_forward, shard):
        self.call_transposed, self.call_forward = call_transposed, call_forward
        self.shard = shard

    def gather_near(self):
        self.middle = self.shard.shape[0] // 2
        parts = [self.shard[: self.middle], self.shard[self.middle :]]
        self.near = [[swap(part, "col", d) for part in parts] for d in (1, 2)]

    def gather_far(self):
        first, second = self.near
        self.pieces = [(0, 0, self.shard)]
        self.pieces += [(d, self.middle * i, part) for d in (1, 2) for i, part in enumerate(self.near[d - 1])]
        self.pieces.append((3, 0, swap(second[0], "col", 1)))
        self.pieces.append((3, self.middle, swap(first[1], "col", 2)))

    def multiply_transposed(self, token=None):
        self.mine, self.other = self.call_transposed(self.pieces, token)

    def send_other(self, token=None):
        self.arrived = swap(after(self.other, token), "row", 1)

    def reduce(self, far):
        rows = lambda value, d: value[d * GROUP : (d + 1) * GROUP]
        self.parts = [rows(self.mine, d) + rows(self.arrived, d) for d in range(3)]
        self.sent = half(self.parts[2] + full(far))
        middle = swap(self.sent, "row", 4)
        self.arriving = [middle]

    def reduce_last(self, token):
        self.arriving.append(swap(half(after(self.parts[1], token)), "row", 2))

    def own(self, token=None):
        middle, low = after(self.arriving, token)
        self.whole = {0: (self.parts[0] + full(middle) + full(low)).astype(jnp.bfloat16)}
        self.whole[2] = swap(self.whole[0], "row", 4)
        self.whole[1] = swap(self.whole[0], "row", 2)

    def spread(self, token=None):
        self.whole[2] = after(self.whole[2], token)
        self.whole[3] = swap(self.whole[2], "row", 2)

    def share(self, token=None):
        self.whole[1], self.whole[3] = after([self.whole[1], self.whole[3]], token)
        near = [self.whole[d] for d in range(4)]
        self.columns = near + [swap(v, "row", 1) for v in near]

    def multiply_forward(self, token=None):
        self.forward = self.call_forward(after(self.columns, token))

    def send_rows(self, token=None):
        self.total, *self.sent = after(self.forward, token)
        self.arrived = [swap(value, "col", d + 1) for d, value in enumerate(self.sent)]

    def finish(self, token=None, *others):
        return finish_call([self.total] + after(self.arrived, token), *others)


def finish_call(parts, *others):
    shape = parts[0].shape
    return pl.pallas_call(
        functools.partial(finish_kernel, len(parts)),
        out_shape=(
            jax.ShapeDtypeStruct(shape, jnp.float32),
            jax.ShapeDtypeStruct((shape[1] * (len(others) + 1), shape[1]), jnp.float32),
        ),
        compiler_params=pltpu.CompilerParams(vmem_limit_bytes=VMEM_LIMIT),
        cost_estimate=NO_COST,
    )(*others, *parts)


def run_pair(call_transposed, a, b, urgent):
    pieces = gather(urgent)
    a.gather_near()
    mine, other = call_transposed(pieces, None)
    arrived = swap(after(other, a.near), "row", 1)
    a.gather_far()
    b.shard = after(b.shard, a.near)
    b.gather_near()
    sent = half(mine + arrived)
    far = swap(sent, "row", 2)
    a.multiply_transposed(sent)
    a.send_other([b.near, far])
    b.gather_far()
    a.reduce(far[:GROUP])
    a.reduce_last([a.sent, [piece[2] for piece in b.pieces[5:]]])
    b.multiply_transposed(a.sent)
    b.send_other(a.arriving[0])
    a.own(b.other)
    b.reduce(after(far[GROUP:], a.whole[0]))
    a.spread(b.sent)
    b.reduce_last(a.whole[3])
    a.share()
    a.multiply_forward()
    b.own(a.forward)
    a.send_rows()
    b.spread()
    b.share(a.arrived[:2])
    b.multiply_forward()
    b.send_rows(a.arrived[2:])


class Sum:
    def __init__(self, value):
        half = value.shape[0] // 2
        self.core = lax.axis_index("row") % 2
        mine = lax.dynamic_slice_in_dim(value, self.core * half, half, 0)
        other = lax.dynamic_slice_in_dim(value, (1 - self.core) * half, half, 0)
        self.mine = mine + swap(other, "row", 1)

    def over_row(self, tokens):
        bit = 2
        while bit < lax.axis_size("row"):
            self.mine = self.mine + after(swap(self.mine, "row", bit), tokens.get(bit))
            bit *= 2

    def over_col(self, token=None):
        mine = after(self.mine, token)
        arrived = [swap(mine, "col", d) for d in range(1, lax.axis_size("col"))]
        stack = jnp.stack([mine] + arrived)
        self.mine = sum(
            lax.dynamic_index_in_dim(stack, lax.axis_index("col") ^ d, 0, keepdims=False)
            for d in range(lax.axis_size("col"))
        )

    def finish(self):
        other = swap(self.mine, "row", 1)
        return jnp.where(
            self.core == 0, jnp.concatenate([self.mine, other]), jnp.concatenate([other, self.mine])
        )


def product(left, right, left_dim, right_dim):
    return lax.dot_general(
        left, right, (((left_dim,), (right_dim,)), ((), ())),
        precision=lax.Precision.HIGHEST, preferred_element_type=jnp.float32,
    )


def finish_kernel(parts, *refs):
    rows_ref, gram_ref = refs[-2:]
    others, parts = refs[: -2 - parts], refs[-2 - parts : -2]
    total = parts[0][...]
    for part in parts[1:]:
        total = total + part[...].astype(jnp.float32)
    rows_ref[...] = total
    size = total.shape[1]
    for i, other in enumerate(others):
        gram_ref[size * i : size * (i + 1), :] = product(other[...], total, 0, 0)
    gram_ref[size * len(others) :, :] = product(total, total, 0, 0)


def factor_with_inverse(matrix):
    size = matrix.shape[1]
    groups = size // SUBLANES
    shape = (SUBLANES, size)
    row = lax.broadcasted_iota(jnp.int32, shape, 0)
    col = lax.broadcasted_iota(jnp.int32, shape, 1)
    left = [matrix[SUBLANES * g : SUBLANES * (g + 1), :] for g in range(groups)]
    right = [(col == row + SUBLANES * g).astype(jnp.float32) for g in range(groups)]
    spread = lambda value, j: jnp.broadcast_to(value[j : j + 1, :], shape)
    for p in range(groups):
        columns = [
            {
                g: jnp.broadcast_to(left[g][:, SUBLANES * p + k : SUBLANES * p + k + 1], shape)
                for g in range(p, groups)
            }
            for k in range(SUBLANES)
        ]
        pivots = None
        for j in range(SUBLANES):
            pivot = spread(columns[j][p], j)
            inverse = 1.0 / pivot
            pivots = pivot if pivots is None else jnp.where(row == j, pivot, pivots)
            left_row, right_row = spread(left[p], j), spread(right[p], j)
            heads = {k: spread(columns[k][p], j) for k in range(j + 1, SUBLANES)}
            for g in range(p, groups):
                scale = columns[j][g] * inverse
                if g == p:
                    scale = jnp.where(row > j, scale, 0.0)
                left[g] = left[g] - scale * left_row
                right[g] = right[g] - scale * right_row
                for k, head in heads.items():
                    columns[k][g] = columns[k][g] - scale * head
        scale = lax.rsqrt(pivots)
        left[p] = jnp.where(col >= row + SUBLANES * p, left[p] * scale, 0.0)
        right[p] = right[p] * scale
    return jnp.concatenate(left), jnp.concatenate(right)


def first_factor_kernel(total_rows, gram_ref, rows_ref, upper_ref, inverse_ref, basis_ref):
    upper, inverse = factor_with_inverse(gram_ref[...] / total_rows)
    upper_ref[...] = upper
    inverse_ref[...] = inverse
    basis_ref[...] = product(rows_ref[...], inverse, 1, 1)


def second_factor_kernel(
    total_rows, gram_ref, upper_ref, inverse_ref, first_ref, rows_ref, basis_ref, factor_ref
):
    split = upper_ref.shape[0]
    mixed, last = gram_ref[:split] / total_rows, gram_ref[split:] / total_rows
    corner = product(inverse_ref[...], mixed, 1, 0)
    upper, inverse = factor_with_inverse(last - product(corner, corner, 0, 0))
    factor_ref[:split, :split] = upper_ref[...]
    factor_ref[:split, split:] = corner
    factor_ref[split:, :split] = jnp.zeros_like(upper)
    factor_ref[split:, split:] = upper
    first = first_ref[...]
    basis_ref[:, :split] = first
    rows = jnp.concatenate([rows_ref[...], first], axis=1)
    blocks = jnp.concatenate([inverse, -product(inverse, corner, 1, 1)], axis=1)
    basis_ref[:, split:] = product(rows, blocks, 1, 1)


def body(tiles, tile_rows, tile_cols, tile_counts, sketch):
    tiles = tiles[0, 0]
    layout = jnp.concatenate([tile_counts[0], tile_rows[0, 0], tile_cols[0, 0]])
    slots, tile_size, _ = tiles.shape
    width, sketch_width = sketch.shape
    group_rows, group_cols = BR * tile_size, BC * tile_size
    split = sketch_width // 2
    rows_axis, cols_axis = lax.axis_size("row"), lax.axis_size("col")

    def call_transposed(pieces, token):
        depth = pieces[0][2].shape[0]
        outs = 2 if rows_axis == 8 else 1
        return tile_call(
            functools.partial(transposed_kernel, [piece[:2] for piece in pieces]),
            [jax.ShapeDtypeStruct((depth // outs, group_cols), jnp.float32)] * outs,
            [pltpu.VMEM((depth, group_rows), jnp.bfloat16)],
            layout, tiles, after([piece[2] for piece in pieces], token),
        )

    def call_forward(columns, outs=cols_axis):
        depth = sum(piece.shape[0] for piece in columns)
        return tile_call(
            functools.partial(forward_kernel, outs),
            [
                jax.ShapeDtypeStruct((group_rows // outs, depth), jnp.bfloat16 if offset else jnp.float32)
                for offset in range(outs)
            ],
            [pltpu.VMEM((depth, group_cols), jnp.bfloat16), pltpu.VMEM((group_rows, depth), jnp.float32)],
            layout, tiles, columns,
        )

    paired = rows_axis == 8 and cols_axis == 4 and sketch_width == 2 * GROUP * rows_axis
    if paired:
        part = lambda groups: jax.ShapeDtypeStruct((groups * GROUP, width), jnp.bfloat16)
        urgent, *halves = pl.pallas_call(
            prepare_kernel,
            out_shape=[part(4), part(6), part(6)],
            scratch_shapes=[pltpu.VMEM((sketch_width, width), jnp.bfloat16)],
            compiler_params=pltpu.CompilerParams(vmem_limit_bytes=VMEM_LIMIT),
            cost_estimate=NO_COST,
        )(sketch)
        a, b = [Half(call_transposed, call_forward, shard) for shard in halves]
        run_pair(call_transposed, a, b, urgent)
        first, first_gram = a.finish(b.sent)
    else:
        everything = lax.all_gather(sketch.T, "col", axis=1, tiled=True)
        (partial,) = call_transposed([(0, 0, everything)], None)
        columns = lax.psum_scatter(partial, "row", scatter_dimension=0, tiled=True).astype(jnp.bfloat16)
        columns = lax.all_gather(columns, "row", axis=0, tiled=True)
        (partial,) = call_forward([columns], 1)
        whole, gram = finish_call([lax.psum_scatter(partial, "col", scatter_dimension=0, tiled=True)])
        first, second = whole[:, :split], whole[:, split:]
        first_gram, mixed_gram = gram[:split, :split], gram[:, split:]
    total_rows = group_rows * lax.axis_size("row")
    params = pltpu.CompilerParams(vmem_limit_bytes=VMEM_LIMIT)
    square = jax.ShapeDtypeStruct((split, split), jnp.float32)
    first_gram = Sum(first_gram)
    first_gram.over_row({2: b.arrived[:1]} if paired else {})
    if paired:
        second, mixed_gram = b.finish(first_gram.mine, first)
    first_gram.over_col()
    mixed_gram = Sum(mixed_gram)
    upper, inverse, first_basis = pl.pallas_call(
        functools.partial(first_factor_kernel, total_rows),
        out_shape=(square, square, jax.ShapeDtypeStruct(first.shape, jnp.float32)),
        compiler_params=params,
    )(first_gram.finish(), first)
    mixed_gram.over_row({4: upper})
    mixed_gram.over_col()
    return pl.pallas_call(
        functools.partial(second_factor_kernel, total_rows),
        out_shape=(
            jax.ShapeDtypeStruct((width, sketch_width), jnp.float32),
            jax.ShapeDtypeStruct((sketch_width, sketch_width), jnp.float32),
        ),
        compiler_params=params,
    )(mixed_gram.finish(), upper, inverse, first_basis, second)


def solution(mesh):
    return jax.shard_map(
        body,
        mesh=mesh,
        in_specs=(
            P("row", "col", None, None, None),
            P("row", "col", None),
            P("row", "col", None),
            P("row", "col"),
            P(("row", "col"), None),
        ),
        out_specs=(P(("row", "col"), None), P()),
        check_vma=False,
    )
```
